256 devices in a mesh: attn: 64 (over x, z, core), tp: 4 (over y).
Axes of the slice: x: 4, y: 4, z: 8, core: 2. Of those that a mesh axis runs over, the one named last changes fastest.
Arguments:
- lengths: int32 [32], replicated, may hold values from 1 to 4, 64 in all
- queries: bfloat16 [32768, 2560], P('attn', 'tp'), may hold values from -8 to 8
- key_vectors: bfloat16 [32768, 512], P('attn', 'tp'), may hold values from -8 to 8
- value_vectors: bfloat16 [32768, 512], P('attn', 'tp'), may hold values from -6 to 6
- out_weight: bfloat16 [2560, 5120], P('tp'), may hold values from -0.125 to 0.125
- grad_output: bfloat16 [32768, 5120], P(('attn', 'tp')), may hold values from -6 to 6
Outputs:
- layer_out: bfloat16 [32768, 5120], P(('attn', 'tp'))
- grad_queries: bfloat16 [32768, 2560], P('attn', 'tp')
- grad_keys: bfloat16 [32768, 512], P('attn', 'tp')
- grad_values: bfloat16 [32768, 512], P('attn', 'tp')
The draws below stay inside these ranges and needn't reach their ends.
Inputs may be any that keep to these rules, and one draw needn't show every extreme that they name: Document d covers lengths[d] whole blocks of 512 tokens; the documents follow one another and fill all 64 blocks; the longest covers exactly 4 blocks.
All inputs are finite; a program needn't handle non-finite values.
Results may differ from the reference program's by a relative error of at most 0.019.
Values may be sent and summed in bfloat16 or wider, within the bound.
A program may use at most 64 MiB of HBM per device.

```python
import math
import jax
import jax.numpy as jnp
import numpy as np
from jax import lax

D = 5120
HEAD_DIM = 128
HEADS = 20
KV_HEADS = 4
TOK_DEV = 512
MOST_CH = 4
GROUP = 5
SPANS = 64
DOCS = 32
TOKENS = 32768
N_TP = 4


def draw_key_vectors(key, part):
    key = jax.random.fold_in(key, 11)
    array_shape = (TOKENS, KV_HEADS, HEAD_DIM)
    sample = jax.random.truncated_normal(key, -6.0, 6.0, array_shape)
    return sample.reshape(TOKENS, KV_HEADS * HEAD_DIM).astype(jnp.bfloat16)


def draw_queries(key, part):
    key = jax.random.fold_in(key, 23)
    array_shape = (TOKENS, KV_HEADS, GROUP, HEAD_DIM)
    sample = jax.random.truncated_normal(key, -6.0, 6.0, array_shape)
    return sample.reshape(TOKENS, KV_HEADS * GROUP * HEAD_DIM).astype(jnp.bfloat16)


def steps_of(own_key, dims, pieces, least, high):
    factor_of, own = 1.0, jax.random.fold_in(own_key, 6)
    for dim, shards_of in pieces:
        heights = jnp.exp(jax.random.uniform(jax.random.fold_in(own, dim), (shards_of,), jnp.float32, least / len(pieces), high / len(pieces)))
        factor_of = factor_of * jnp.repeat(heights, dims[dim] // shards_of).reshape([-1 if axis == dim else 1 for axis in range(len(dims))])
    return factor_of


def split_up(number_of, total, reach, lean):
    portions = [(1 << 20) // math.isqrt(rank ** lean) + 1 for rank in range(2, number_of + 1)]
    spare, counts = total - reach - (number_of - 1), [1] * (number_of - 1)
    while spare > 0:
        free = [i for i in range(number_of - 1) if counts[i] < reach]
        mass, left = sum([portions[i] for i in free]), spare
        for i in free:
            addition = min(reach - counts[i], max(1, left * portions[i] // mass), spare)
            counts[i] = counts[i] + addition
            spare = spare - addition
    return np.array([reach] + counts)


def uneven_parts(own_key, amount, total, reach, skew):
    if amount == 2:
        one = jax.random.randint(own_key, (), max(1, total - reach), min(reach, total - 1) + 1)
        return jnp.stack([one, total - one])
    tallies = jnp.asarray(split_up(amount, total, reach, skew), jnp.int32)
    twos = (amount - 1) // 2
    donor, receiver = tallies[1:1 + 2 * twos:2], tallies[2:2 + 2 * twos:2]
    room = jnp.minimum(donor - 1, reach - receiver)
    moved = jax.random.randint(jax.random.fold_in(own_key, 1), (twos,), 0, 1 << 20) % (room + 1)
    tallies = tallies.at[1:1 + 2 * twos:2].set(donor - moved).at[2:2 + 2 * twos:2].set(receiver + moved)
    return tallies[jax.random.permutation(jax.random.fold_in(own_key, 2), amount)]


def bell_draw(key, shape, deviation, reach, cuts=(), kind=jnp.bfloat16):
    loudness = steps_of(key, shape, cuts, -0.22, 0.18) if cuts else 1.0
    drawn = jax.random.normal(key, shape, jnp.float32) * deviation * loudness
    return jnp.minimum(jnp.maximum(drawn, -reach), reach).astype(kind)


def setup_inputs(seed: int = 0) -> dict:
    keys = jax.random.split(jax.random.key(seed), 7)
    return {
        "lengths": uneven_parts(keys[0], DOCS, SPANS, MOST_CH, 2).astype(jnp.int32),
        "queries": draw_queries(jax.random.fold_in(keys[6], 71), 0),
        "key_vectors": draw_key_vectors(jax.random.fold_in(keys[6], 71), 0),
        "value_vectors": bell_draw(keys[3], (TOKENS, KV_HEADS * HEAD_DIM), 1.0, 6.0, ((0, 64), (1, 4))),
        "out_weight": bell_draw(keys[4], (HEADS * HEAD_DIM, D), (HEADS * HEAD_DIM) ** -0.5, 0.125, ((0, 4),)),
        "grad_output": bell_draw(keys[5], (TOKENS, D), 1.0, 6.0, ((0, 256),)),
    }


NEGATIVE = -1e30


def widen(array):
    return lax.optimization_barrier(array).astype(jnp.float32)


def masked_scores(query_blk, key_blk, offset):
    tok = query_blk.shape[0]
    logits = jnp.einsum("tgrd,ugd->grtu", widen(query_blk), widen(key_blk)) * (HEAD_DIM ** -0.5)
    rows_at = lax.broadcasted_iota(jnp.int32, (tok, tok), 0)
    cols_at = lax.broadcasted_iota(jnp.int32, (tok, tok), 1)
    keep = (offset > 0) | (cols_at <= rows_at)
    return jnp.where(keep, logits, NEGATIVE)


def block_depths(lengths):
    ends = jnp.cumsum(lengths).astype(jnp.int32)
    blocks = jnp.arange(SPANS, dtype=jnp.int32)
    owner = jnp.sum((blocks[:, None] >= ends[None, :]).astype(jnp.int32), axis=1)
    starts = ends - lengths
    docs_at = jnp.arange(DOCS, dtype=jnp.int32)
    first = jnp.sum(jnp.where(owner[:, None] == docs_at[None, :], starts[None, :], 0), axis=1)
    return (blocks - first).astype(jnp.int32)


def span_stats(query_blk, fetch, depth):
    stat_shape = (query_blk.shape[1], query_blk.shape[2], query_blk.shape[0])

    def step(offset, carry):
        def live(carry):
            top, total = carry
            key_blk, value_blk = fetch(offset)
            logits = masked_scores(query_blk, key_blk, offset)
            new_top = jnp.maximum(top, jnp.max(logits, axis=-1))
            total = total * jnp.exp(top - new_top) + jnp.sum(jnp.exp(logits - new_top[..., None]), axis=-1)
            return new_top, total

        def skipped(carry):
            return carry

        return lax.cond(offset <= depth, live, skipped, carry)

    start = (jnp.full(stat_shape, NEGATIVE, jnp.float32), jnp.zeros(stat_shape, jnp.float32))
    top, total = lax.fori_loop(0, MOST_CH, step, start)
    return top + jnp.log(total)


def span_output(query_blk, fetch, depth, log_total):
    def step(offset, accum):
        def live(accum):
            key_blk, value_blk = fetch(offset)
            logits = masked_scores(query_blk, key_blk, offset)
            weights = jnp.exp(logits - log_total[..., None]).astype(jnp.bfloat16)
            return accum + jnp.einsum("grtu,ugd->tgrd", widen(weights), widen(value_blk))

        def skipped(accum):
            return accum

        return lax.cond(offset <= depth, live, skipped, accum)

    accum = lax.fori_loop(0, MOST_CH, step, jnp.zeros(query_blk.shape, jnp.float32))
    return accum.astype(jnp.bfloat16)


def task_grads(query_blk, grad_blk, log_total, delta, key_blk, value_blk, offset):
    logits = masked_scores(query_blk, key_blk, offset)
    probs = jnp.exp(logits - log_total[..., None])
    probs_low = probs.astype(jnp.bfloat16)
    dprobs = jnp.einsum("tgrd,ugd->grtu", widen(grad_blk), widen(value_blk))
    dlogits = (probs * (dprobs - delta[..., None])).astype(jnp.bfloat16)
    grad_q = jnp.einsum("grtu,ugd->tgrd", widen(dlogits), widen(key_blk))
    grad_k = jnp.einsum("grtu,tgrd->ugd", widen(dlogits), widen(query_blk)) * (HEAD_DIM ** -0.5)
    grad_v = jnp.einsum("grtu,tgrd->ugd", widen(probs_low), widen(grad_blk))
    return grad_q, grad_k, grad_v


def reference(lengths, queries, key_vectors, value_vectors, out_weight, grad_output):
    depths = block_depths(lengths)
    blocked = queries.reshape(SPANS, TOK_DEV, KV_HEADS, GROUP, HEAD_DIM)
    margin = (MOST_CH - 1) * TOK_DEV
    key_pad = jnp.concatenate([jnp.zeros((margin, KV_HEADS * HEAD_DIM), key_vectors.dtype), key_vectors], axis=0)
    key_pad = key_pad.reshape(margin + TOKENS, KV_HEADS, HEAD_DIM)
    value_pad = jnp.concatenate([jnp.zeros((margin, KV_HEADS * HEAD_DIM), value_vectors.dtype), value_vectors], axis=0)
    value_pad = value_pad.reshape(margin + TOKENS, KV_HEADS, HEAD_DIM)

    def fetcher(block):
        def fetch(offset):
            where_at = ((block - offset + MOST_CH - 1) * TOK_DEV).astype(jnp.int32)
            return (lax.dynamic_slice_in_dim(key_pad, where_at, TOK_DEV, 0),
                    lax.dynamic_slice_in_dim(value_pad, where_at, TOK_DEV, 0))
        return fetch

    def forward(block):
        query_blk = blocked[block]
        fetch = fetcher(block)
        log_total = span_stats(query_blk, fetch, depths[block])
        return span_output(query_blk, fetch, depths[block], log_total), log_total

    outputs, totals = lax.map(forward, jnp.arange(SPANS, dtype=jnp.int32))
    attn_out = outputs.reshape(TOKENS, HEADS * HEAD_DIM)
    width = HEADS * HEAD_DIM // N_TP
    summed = jnp.zeros((TOKENS, D), jnp.float32)
    for group_index in range(N_TP):
        partial_out = jnp.dot(attn_out[:, group_index * width:(group_index + 1) * width],
                              out_weight[group_index * width:(group_index + 1) * width],
                              preferred_element_type=jnp.float32).astype(jnp.bfloat16)
        summed = summed + partial_out.astype(jnp.float32)
    layer_out = summed.astype(jnp.bfloat16)
    grad_attn = jnp.dot(grad_output, out_weight.T, preferred_element_type=jnp.float32).astype(jnp.bfloat16)
    grad_blocks = grad_attn.reshape(SPANS, TOK_DEV, KV_HEADS, GROUP, HEAD_DIM)

    def backward(carry, block):
        query_blk = blocked[block]
        grad_blk = grad_blocks[block]
        out_blk = outputs[block]
        delta = jnp.transpose(jnp.sum(widen(grad_blk) * widen(out_blk), axis=-1), (1, 2, 0))
        log_total = totals[block]
        fetch = fetcher(block)
        depth = depths[block]

        def step(offset, inner):
            def live(inner):
                grad_q, keys_acc, values_acc = inner
                key_blk, value_blk = fetch(offset)
                part_q, part_k, part_v = task_grads(query_blk, grad_blk, log_total, delta, key_blk, value_blk, offset)
                where_at = ((block - offset + MOST_CH - 1) * TOK_DEV).astype(jnp.int32)
                keys_acc = lax.dynamic_update_slice_in_dim(
                    keys_acc, lax.dynamic_slice_in_dim(keys_acc, where_at, TOK_DEV, 0) + part_k, where_at, 0)
                values_acc = lax.dynamic_update_slice_in_dim(
                    values_acc, lax.dynamic_slice_in_dim(values_acc, where_at, TOK_DEV, 0) + part_v, where_at, 0)
                return grad_q + part_q, keys_acc, values_acc

            def skipped(inner):
                return inner

            return lax.cond(offset <= depth, live, skipped, inner)

        grad_q, keys_acc, values_acc = lax.fori_loop(
            0, MOST_CH, step, (jnp.zeros(query_blk.shape, jnp.float32), carry[0], carry[1]))
        result = (grad_q * (HEAD_DIM ** -0.5)).astype(jnp.bfloat16).reshape(TOK_DEV, HEADS * HEAD_DIM)
        return (keys_acc, values_acc), result

    empty = jnp.zeros((margin + TOKENS, KV_HEADS, HEAD_DIM), jnp.float32)
    (keys_acc, values_acc), grads_q = lax.scan(backward, (empty, empty), jnp.arange(SPANS, dtype=jnp.int32))
    grad_queries = grads_q.reshape(TOKENS, HEADS * HEAD_DIM)
    grad_keys = keys_acc[margin:].reshape(TOKENS, KV_HEADS * HEAD_DIM).astype(jnp.bfloat16)
    grad_values = values_acc[margin:].reshape(TOKENS, KV_HEADS * HEAD_DIM).astype(jnp.bfloat16)
    return layer_out, grad_queries, grad_keys, grad_values
```

```python
import functools

import jax
import jax.numpy as jnp
from jax import lax
from jax.experimental import pallas as pl
from jax.experimental.pallas import tpu as pltpu
from jax.sharding import PartitionSpec as P

HD = 128
REACH = 4
GROUP = 5
N_TP = 4
PARTS = 8
CHUNKS = 4
NEGATIVE = -1e30
SCALE = HD ** (-0.5)
LOG2E = 1.4426950408889634
MESH = pl.DeviceIdType.MESH
BF, F32 = jnp.bfloat16, jnp.float32


def dot(a, b):
    return jnp.dot(a, b, preferred_element_type=F32)


def dot_nt(a, b):
    return lax.dot_general(a, b, (((1,), (1,)), ((), ())), preferred_element_type=F32)


def kernel(
    n,
    docs,
    len_ref,
    q_ref,
    k_ref,
    v_ref,
    w_ref,
    go_ref,
    lo_ref,
    gq_ref,
    gk_ref,
    gv_ref,
    qh,
    qt,
    kb,
    vb,
    kt,
    vt,
    wm,
    wp,
    go,
    acc,
    stat_m,
    stat_l,
    ot,
    o_all,
    op,
    rs_send,
    rs_recv,
    lo_acc,
    lo_out,
    dot_acc,
    dot_own,
    dot_rem,
    dot_send,
    d_own,
    d_rem,
    delta,
    dk_acc,
    dv_acc,
    dq_acc,
    dkv_send,
    dkv_recv,
    gq_out,
    gk_out,
    gv_out,
    tabs_ref,
    loc_sem,
    out_sem,
    send_sem,
    recv_sem,
):
    tok, width = q_ref.shape
    row = tok // N_TP
    two = 2 * row
    feat = go_ref.shape[1]
    half = feat // 2
    me, y = lax.axis_index("attn"), lax.axis_index("tp")
    step_x = n // 4
    core = lax.rem(me, 2)
    x = me // step_x
    y_a = y + 1 - 2 * lax.rem(y, 2)
    y_b = N_TP - 1 - y
    perm = [y, y_b, y_a, N_TP - 1 - y_a]

    def at(shift):
        return (lax.rem(me + shift + n, n), y)

    dev_a, dev_b = (me, y_a), (me, y_b)
    x_up, x_down = at(step_x), at(-step_x)
    sib = (me + 1 - 2 * core, y)

    def part_of(shift):
        return lax.rem(x + shift + 4, 4) * 2 + core

    partners = [at(s) for s in (1, 2, 3, -1, -2, -3)] + [dev_a, dev_b, x_up, x_down]
    barrier = pltpu.get_barrier_semaphore()
    for dev in partners:
        pl.semaphore_signal(barrier, inc=1, device_id=dev, device_id_type=MESH)

    def local(i, src, dst):
        c = pltpu.make_async_copy(src, dst, loc_sem.at[i])
        c.start()
        return c

    loc_k = local(0, k_ref, kb.at[0])
    loc_v = local(1, v_ref, vb.at[0])
    loc_q = []
    for s in range(N_TP):
        rows = pl.ds(pl.multiple_of(perm[s] * row, row), row)
        for h in range(GROUP):
            loc_q.append(
                local(
                    2 + s * GROUP + h,
                    q_ref.at[rows, pl.ds(h * HD, HD)],
                    qh.at[h, pl.ds(s * row, row)],
                )
            )
    loc_go = local(2 + N_TP * GROUP, go_ref, go.at[0])
    loc_w = local(3 + N_TP * GROUP, w_ref, wm)

    pl.semaphore_wait(barrier, len(partners))

    used = [0]

    def remote(src, dst, dev):
        i = used[0]
        used[0] += 1
        c = pltpu.make_async_remote_copy(
            src_ref=src,
            dst_ref=dst,
            send_sem=send_sem.at[i],
            recv_sem=recv_sem.at[i],
            device_id=dev,
            device_id_type=MESH,
        )
        c.start()
        return c

    sides = [pl.ds(0, half), pl.ds(half, half)]
    mine = part_of(0)
    kv = [None]
    kv.append((remote(k_ref, kb.at[1], at(1)), remote(v_ref, vb.at[1], at(1))))
    wa = [remote(w_ref.at[mine, :, sides[0]], wp.at[mine, :, sides[0]], dev_a)]
    kv.append((remote(k_ref, kb.at[2], at(2)), remote(v_ref, vb.at[2], at(2))))
    kv.append((remote(k_ref, kb.at[3], at(3)), remote(v_ref, vb.at[3], at(3))))
    wa.append(remote(w_ref.at[mine, :, sides[1]], wp.at[mine, :, sides[1]], dev_a))
    go_b = remote(go_ref, go.at[1], dev_b)

    end, first = jnp.int32(0), jnp.int32(0)
    for d in range(docs):
        end = end + len_ref[d]
        first = jnp.where(end <= me, end, first)
    depth = me - first
    bias = [jnp.where(o <= depth, 0.0, -NEGATIVE).astype(F32) for o in range(REACH)]

    lane = lax.broadcasted_iota(jnp.int32, (1, row), 1)
    for s in range(N_TP):
        tabs_ref[:, s * row : (s + 1) * row] = lane + perm[s] * row

    c2 = SCALE * LOG2E

    for c in loc_q:
        c.wait()

    def turn_q(h, carry):
        qt[h] = qh[h].T
        return carry

    lax.fori_loop(0, GROUP, turn_q, 0)

    def turn_kv(o):
        kt[o] = kb[o].T
        vt[o] = vb[o].T

    def forward(o):
        turn_kv(o)

        def head(h, carry):
            s = dot(kb[o], qt[h])
            if o == 0:
                at_u = lax.broadcasted_iota(jnp.int32, (tok, tok), 0)
                s = jnp.where(at_u <= tabs_ref[...], s, NEGATIVE)
                new = jnp.max(s, axis=0, keepdims=True)
                p = jnp.exp2((s - new) * c2)
                stat_l[h] = jnp.sum(p, axis=0, keepdims=True)
                acc[h] = dot(vt[o], p.astype(BF))
            else:
                old = stat_m[h]
                new = jnp.maximum(old, jnp.max(s, axis=0, keepdims=True) - bias[o])
                fade = jnp.exp2((old - new) * c2)
                p = jnp.exp2((s - (new + bias[o])) * c2)
                stat_l[h] = stat_l[h] * fade + jnp.sum(p, axis=0, keepdims=True)
                acc[h] = acc[h] * fade + dot(vt[o], p.astype(BF))
            stat_m[h] = new
            return carry

        lax.fori_loop(0, GROUP, head, 0)

    loc_k.wait()
    loc_v.wait()
    forward(0)
    for c in kv[1]:
        c.wait_recv()
    forward(1)

    wa[0].wait_recv()
    piece = wp.at[mine, :, sides[0]]
    up0 = remote(piece, piece, x_up)
    down0 = remote(piece, piece, x_down)
    sibs = [remote(piece, piece, sib)]

    for c in kv[2]:
        c.wait_recv()
    forward(2)

    wa[1].wait_recv()
    piece = wp.at[mine, :, sides[1]]
    up1 = remote(piece, piece, x_up)
    down1 = remote(piece, piece, x_down)
    sibs.append(remote(piece, piece, sib))

    for c in kv[3]:
        c.wait_recv()
    forward(3)

    for h in range(GROUP):
        low = (acc[h] * (1.0 / stat_l[h])).astype(BF)
        ot[h] = low
        o_all[:, h * HD : (h + 1) * HD] = low.T
        stat_l[h] = stat_m[h] * c2 + jnp.log2(stat_l[h])
    o_a = remote(o_all.at[pl.ds(two, two)], op, dev_a)

    from_down, from_up, from_far = part_of(-1), part_of(1), part_of(2)
    up0.wait_recv()
    piece = wp.at[from_down, :, sides[0]]
    far_up = remote(piece, piece, x_up)
    sibs.append(remote(piece, piece, sib))
    down0.wait_recv()
    piece = wp.at[from_up, :, sides[0]]
    sibs.append(remote(piece, piece, sib))

    def cotangent(w3, out):
        dot_acc[...] = jnp.zeros_like(dot_acc)
        deep = feat // CHUNKS

        def step(j, carry):
            cols = pl.ds(pl.multiple_of(j * deep, deep), deep)
            part = w3[:, :, cols].reshape(width, deep)
            for s in range(2):
                dot_acc[:, s * row : (s + 1) * row] += dot_nt(part, go[s, :, cols])
            return carry

        lax.fori_loop(0, CHUNKS, step, 0)
        for h in range(GROUP):
            out[h] = dot_acc[h * HD : (h + 1) * HD, :].astype(BF)

    def turn_d(src, dst, base):
        def head(h, carry):
            high = src[h]
            dst[h] = high.T
            delta[h, :, pl.ds(base, two)] = jnp.sum(
                high.astype(F32) * ot[h, :, pl.ds(base, two)].astype(F32), axis=0, keepdims=True
            )
            return carry

        lax.fori_loop(0, GROUP, head, 0)

    loc_w.wait()
    loc_go.wait()
    go_b.wait_recv()
    cotangent(wm, dot_own)
    turn_d(dot_own, d_own, 0)

    up1.wait_recv()
    piece = wp.at[from_down, :, sides[1]]
    sibs.append(remote(piece, piece, sib))
    down1.wait_recv()
    piece = wp.at[from_up, :, sides[1]]
    far_down = remote(piece, piece, x_down)
    sibs.append(remote(piece, piece, sib))

    def backward(o, base, dt, dd, fresh):
        tl = pl.ds(base, two)

        def head(h, carry):
            s = dot(kb[o], qt[h, :, tl])
            p = jnp.exp2(s * c2 - (stat_l[h, :, tl] + bias[o]))
            if o == 0:
                at_u = lax.broadcasted_iota(jnp.int32, (tok, two), 0)
                p = jnp.where(at_u <= tabs_ref[:, tl], p, 0.0)
            dp = dot(vb[o], dt[h])
            ds = (p * (dp - delta[h, :, tl])).astype(BF)
            dv_acc[o] += dot(p.astype(BF), dd[h])
            dk_acc[o] += dot(ds, qh[h, tl])
            part_q = dot(kt[o], ds)
            if o == REACH - 1:
                dq_acc[h, :, tl] = part_q
            else:
                dq_acc[h, :, tl] += part_q
            return carry

        if fresh:
            dv_acc[o] = jnp.zeros((tok, HD), F32)
            dk_acc[o] = jnp.zeros((tok, HD), F32)
        lax.fori_loop(0, GROUP, head, 0)

    for o in range(REACH - 1, -1, -1):
        backward(o, 0, dot_own, d_own, True)

    far_up.wait_recv()
    piece = wp.at[from_far, :, sides[0]]
    sibs.append(remote(piece, piece, sib))
    far_down.wait_recv()
    piece = wp.at[from_far, :, sides[1]]
    sibs.append(remote(piece, piece, sib))
    for c in sibs:
        c.wait_recv()
    o_a.wait_recv()

    wide = feat // CHUNKS
    rs = []
    for j in range(CHUNKS):
        cols = slice(j * wide, (j + 1) * wide)
        one = dot(o_all[0:two], wm[:, :, cols].reshape(width, wide)).astype(BF)
        other = dot(op[...], wp[:, :, cols].reshape(width, wide)).astype(BF)
        both = one.astype(F32) + other.astype(F32)
        lo_acc[:, cols] = both[0:row]
        rs_send[:, cols] = both[row:two].astype(BF)
        span = pl.ds(j * wide, wide)
        rs.append(remote(rs_send.at[:, span], rs_recv.at[:, span], dev_b))

    cotangent(wp, dot_send)
    d_a = remote(dot_send, dot_rem, dev_a)
    d_a.wait_recv()
    turn_d(dot_rem, d_rem, two)

    back = []
    for o in range(REACH - 1, -1, -1):
        backward(o, two, dot_rem, d_rem, False)
        if o > 0:
            dkv_send[o - 1, :, 0:HD] = (dk_acc[o] * SCALE).astype(BF)
            dkv_send[o - 1, :, HD : 2 * HD] = dv_acc[o].astype(BF)
            back.append(remote(dkv_send.at[o - 1], dkv_recv.at[o - 1], at(-o)))

    outs = []

    def put(src, dst):
        c = pltpu.make_async_copy(src, dst, out_sem.at[len(outs)])
        c.start()
        outs.append(c)

    for h in range(GROUP):
        gq_out[:, h * HD : (h + 1) * HD] = (dq_acc[h] * SCALE).T.astype(BF)
    for s in range(N_TP):
        rows = pl.ds(pl.multiple_of(perm[s] * row, row), row)
        put(gq_out.at[pl.ds(s * row, row)], gq_ref.at[rows])

    for c in rs:
        c.wait_recv()
    lo_out[...] = (lo_acc[...] + rs_recv[...].astype(F32)).astype(BF)
    put(lo_out, lo_ref)

    for c in back:
        c.wait_recv()
    gk = dk_acc[0] * SCALE
    gv = dv_acc[0]
    for o in range(1, REACH):
        gk = gk + dkv_recv[o - 1, :, 0:HD].astype(F32)
        gv = gv + dkv_recv[o - 1, :, HD : 2 * HD].astype(F32)
    gk_out[...] = gk.astype(BF)
    gv_out[...] = gv.astype(BF)
    put(gk_out, gk_ref)
    put(gv_out, gv_ref)

    sent = [c for pair in kv[1:] for c in pair] + wa + [go_b, up0, down0, up1, down1]
    sent += sibs + [far_up, far_down, o_a, d_a] + rs + back
    for c in sent:
        c.wait_send()
    for c in outs:
        c.wait()


def on_device(n, lengths, queries, key_vectors, value_vectors, out_weight, grad_output):
    tok, width = queries.shape
    feat = out_weight.shape[1]
    row, two = tok // N_TP, tok // 2
    docs = lengths.shape[0]
    hbm = pl.BlockSpec(memory_space=pl.ANY)
    vm = pltpu.VMEM
    dma = pltpu.SemaphoreType.DMA
    flops = 2 * tok * width * feat * 2 + 7 * 2 * tok * tok * width * REACH
    return pl.pallas_call(
        functools.partial(kernel, n, docs),
        out_shape=(
            jax.ShapeDtypeStruct((row, feat), BF),
            jax.ShapeDtypeStruct((tok, width), BF),
            jax.ShapeDtypeStruct((tok, HD), BF),
            jax.ShapeDtypeStruct((tok, HD), BF),
        ),
        in_specs=[pl.BlockSpec(memory_space=pltpu.SMEM)] + [hbm] * 5,
        out_specs=(hbm,) * 4,
        scratch_shapes=[
            vm((GROUP, tok, HD), BF),
            vm((GROUP, HD, tok), BF),
            vm((REACH, tok, HD), BF),
            vm((REACH, tok, HD), BF),
            vm((REACH, HD, tok), BF),
            vm((REACH, HD, tok), BF),
            vm((PARTS, width // PARTS, feat), BF),
            vm((PARTS, width // PARTS, feat), BF),
            vm((2, row, feat), BF),
            vm((GROUP, HD, tok), F32),
            vm((GROUP, 1, tok), F32),
            vm((GROUP, 1, tok), F32),
            vm((GROUP, HD, tok), BF),
            vm((tok, width), BF),
            vm((two, width), BF),
            vm((row, feat), BF),
            vm((row, feat), BF),
            vm((row, feat), F32),
            vm((row, feat), BF),
            vm((width, two), F32),
            vm((GROUP, HD, two), BF),
            vm((GROUP, HD, two), BF),
            vm((GROUP, HD, two), BF),
            vm((GROUP, two, HD), BF),
            vm((GROUP, two, HD), BF),
            vm((GROUP, 1, tok), F32),
            vm((REACH, tok, HD), F32),
            vm((REACH, tok, HD), F32),
            vm((GROUP, HD, tok), F32),
            vm((REACH - 1, tok, 2 * HD), BF),
            vm((REACH - 1, tok, 2 * HD), BF),
            vm((tok, width), BF),
            vm((tok, HD), BF),
            vm((tok, HD), BF),
            vm((1, tok), jnp.int32),
            dma((4 + N_TP * GROUP,)),
            dma((7,)),
            dma((40,)),
            dma((40,)),
        ],
        compiler_params=pltpu.CompilerParams(
            collective_id=0, has_side_effects=True, vmem_limit_bytes=56 * 1024 * 1024
        ),
        cost_estimate=pl.CostEstimate(flops=flops, bytes_accessed=1 << 24, transcendentals=1 << 23),
    )(
        lengths,
        queries,
        key_vectors,
        value_vectors,
        out_weight.reshape(PARTS, width // PARTS, feat),
        grad_output,
    )


def solution(mesh):
    return jax.shard_map(
        functools.partial(on_device, mesh.shape["attn"]),
        mesh=mesh,
        in_specs=(
            P(),
            P("attn", "tp"),
            P("attn", "tp"),
            P("attn", "tp"),
            P("tp", None),
            P(("attn", "tp"), None),
        ),
        out_specs=(P(("attn", "tp"), None), P("attn", "tp"), P("attn", "tp"), P("attn", "tp")),
        check_vma=False,
    )
```

```python
import functools

import jax
import jax.numpy as jnp
from jax import lax
from jax.experimental import pallas as pl
from jax.experimental.pallas import tpu as pltpu
from jax.sharding import PartitionSpec as P

HD = 128
REACH = 4
GROUP = 5
N_TP = 4
PARTS = 8
CHUNKS = 4
NEGATIVE = -1e30
SCALE = HD ** (-0.5)
LOG2E = 1.4426950408889634
MESH = pl.DeviceIdType.MESH
BF, F32 = jnp.bfloat16, jnp.float32


def dot(a, b):
    return jnp.dot(a, b, preferred_element_type=F32)


def dot_nt(a, b):
    return lax.dot_general(a, b, (((1,), (1,)), ((), ())), preferred_element_type=F32)


def kernel(
    n,
    docs,
    len_ref,
    q_ref,
    k_ref,
    v_ref,
    w_ref,
    go_ref,
    lo_ref,
    gq_ref,
    gk_ref,
    gv_ref,
    qh,
    qt,
    kb,
    vb,
    kt,
    vt,
    wm,
    wp,
    go,
    acc,
    stat_m,
    stat_l,
    ot,
    o_all,
    op,
    rs_send,
    rs_recv,
    lo_acc,
    lo_out,
    dot_acc,
    dot_acc_a,
    dot_own,
    dot_rem,
    dot_send,
    d_own,
    d_rem,
    delta,
    dk_acc,
    dv_acc,
    dq_acc,
    dkv_send,
    dkv_recv,
    gq_out,
    gk_out,
    gv_out,
    tabs_ref,
    loc_sem,
    out_sem,
    send_sem,
    recv_sem,
):
    tok, width = q_ref.shape
    row = tok // N_TP
    two = 2 * row
    feat = go_ref.shape[1]
    me, y = lax.axis_index("attn"), lax.axis_index("tp")
    step_x = n // 4
    core = lax.rem(me, 2)
    x = me // step_x
    y_a = y + 1 - 2 * lax.rem(y, 2)
    y_b = N_TP - 1 - y
    perm = [y, y_b, y_a, N_TP - 1 - y_a]

    def at(shift):
        return (lax.rem(me + shift + n, n), y)

    dev_a, dev_b = (me, y_a), (me, y_b)
    x_up, x_down = at(step_x), at(-step_x)
    sib = (me + 1 - 2 * core, y)

    def part_of(shift):
        return lax.rem(x + shift + 4, 4) * 2 + core

    partners = [at(s) for s in (1, 2, 3, -1, -2, -3)] + [dev_a, dev_b, x_up, x_down]
    barrier = pltpu.get_barrier_semaphore()
    for dev in partners:
        pl.semaphore_signal(barrier, inc=1, device_id=dev, device_id_type=MESH)

    def local(i, src, dst):
        c = pltpu.make_async_copy(src, dst, loc_sem.at[i])
        c.start()
        return c

    loc_k = local(0, k_ref, kb.at[0])
    loc_v = local(1, v_ref, vb.at[0])
    loc_q = []
    for s in range(N_TP):
        rows = pl.ds(pl.multiple_of(perm[s] * row, row), row)
        for h in range(GROUP):
            loc_q.append(
                local(
                    2 + s * GROUP + h,
                    q_ref.at[rows, pl.ds(h * HD, HD)],
                    qh.at[h, pl.ds(s * row, row)],
                )
            )
    loc_go = local(2 + N_TP * GROUP, go_ref, go.at[0])
    loc_w = local(3 + N_TP * GROUP, w_ref, wm)

    pl.semaphore_wait(barrier, len(partners))

    used = [0]

    def remote(src, dst, dev):
        i = used[0]
        used[0] += 1
        c = pltpu.make_async_remote_copy(
            src_ref=src,
            dst_ref=dst,
            send_sem=send_sem.at[i],
            recv_sem=recv_sem.at[i],
            device_id=dev,
            device_id_type=MESH,
        )
        c.start()
        return c

    wide = feat // CHUNKS
    cols = [pl.ds(j * wide, wide) for j in range(CHUNKS)]
    mine, from_down, from_up, from_far = [part_of(s) for s in (0, -1, 1, 2)]
    kv = [None, (remote(k_ref, kb.at[1], at(1)), remote(v_ref, vb.at[1], at(1)))]
    wa, go_b = [], []
    for j in range(CHUNKS):
        wa.append(remote(w_ref.at[mine, :, cols[j]], wp.at[mine, :, cols[j]], dev_a))
        go_b.append(remote(go_ref.at[:, cols[j]], go.at[1, :, cols[j]], dev_b))

    up, down, far = {}, {}, {}
    sibs = [[] for _ in range(CHUNKS)]

    def pass_own(j):
        wa[j].wait_recv()
        piece = wp.at[mine, :, cols[j]]
        up[j] = remote(piece, piece, x_up)
        down[j] = remote(piece, piece, x_down)
        sibs[j].append(remote(piece, piece, sib))

    def pass_near(j):
        up[j].wait_recv()
        piece = wp.at[from_down, :, cols[j]]
        if j % 2 == 0:
            far[j] = remote(piece, piece, x_up)
        sibs[j].append(remote(piece, piece, sib))
        down[j].wait_recv()
        piece = wp.at[from_up, :, cols[j]]
        if j % 2 == 1:
            far[j] = remote(piece, piece, x_down)
        sibs[j].append(remote(piece, piece, sib))

    def pass_far(j):
        far[j].wait_recv()
        piece = wp.at[from_far, :, cols[j]]
        sibs[j].append(remote(piece, piece, sib))

    def have(j):
        for c in sibs[j]:
            c.wait_recv()

    def next_keys(o):
        for c in kv[o]:
            c.wait_recv()
        if o < REACH - 1:
            kv.append(
                (
                    remote(kb.at[o], kb.at[o + 1], at(1)),
                    remote(vb.at[o], vb.at[o + 1], at(1)),
                )
            )

    end, first = jnp.int32(0), jnp.int32(0)
    for d in range(docs):
        end = end + len_ref[d]
        first = jnp.where(end <= me, end, first)
    depth = me - first
    bias = [jnp.where(o <= depth, 0.0, -NEGATIVE).astype(F32) for o in range(REACH)]

    lane = lax.broadcasted_iota(jnp.int32, (1, row), 1)
    for s in range(N_TP):
        tabs_ref[:, s * row : (s + 1) * row] = lane + perm[s] * row

    c2 = SCALE * LOG2E

    for c in loc_q:
        c.wait()

    def turn_q(h, carry):
        qt[h] = qh[h].T
        return carry

    lax.fori_loop(0, GROUP, turn_q, 0)

    def turn_kv(o):
        kt[o] = kb[o].T
        vt[o] = vb[o].T

    def forward(o):
        turn_kv(o)

        def head(h, carry):
            s = dot(kb[o], qt[h])
            if o == 0:
                at_u = lax.broadcasted_iota(jnp.int32, (tok, tok), 0)
                s = jnp.where(at_u <= tabs_ref[...], s, NEGATIVE)
                new = jnp.max(s, axis=0, keepdims=True)
                p = jnp.exp2((s - new) * c2)
                stat_l[h] = jnp.sum(p, axis=0, keepdims=True)
                acc[h] = dot(vt[o], p.astype(BF))
            else:
                old = stat_m[h]
                new = jnp.maximum(old, jnp.max(s, axis=0, keepdims=True) - bias[o])
                fade = jnp.exp2((old - new) * c2)
                p = jnp.exp2((s - (new + bias[o])) * c2)
                stat_l[h] = stat_l[h] * fade + jnp.sum(p, axis=0, keepdims=True)
                acc[h] = acc[h] * fade + dot(vt[o], p.astype(BF))
            stat_m[h] = new
            return carry

        lax.fori_loop(0, GROUP, head, 0)

    loc_k.wait()
    loc_v.wait()
    forward(0)
    next_keys(1)
    forward(1)
    pass_own(0)
    next_keys(2)
    forward(2)
    pass_own(1)
    next_keys(3)
    forward(3)

    for h in range(GROUP):
        low = (acc[h] * (1.0 / stat_l[h])).astype(BF)
        ot[h] = low
        o_all[:, h * HD : (h + 1) * HD] = low.T
        stat_l[h] = stat_m[h] * c2 + jnp.log2(stat_l[h])
    o_a = remote(o_all.at[pl.ds(two, two)], op, dev_a)

    def cotangent(w3, total, j):
        part = dot_nt(
            w3[:, :, cols[j]].reshape(width, wide), go[:, :, cols[j]].reshape(two, wide)
        )
        if j == 0:
            total[...] = part
        else:
            total[...] += part

    def heads_of(total, out):
        for h in range(GROUP):
            out[h] = total[h * HD : (h + 1) * HD, :].astype(BF)

    rs = []

    def project(j):
        one = dot(o_all[0:two], wm[:, :, cols[j]].reshape(width, wide)).astype(BF)
        other = dot(op[...], wp[:, :, cols[j]].reshape(width, wide)).astype(BF)
        both = one.astype(F32) + other.astype(F32)
        lo_acc[:, cols[j]] = both[0:row]
        rs_send[:, cols[j]] = both[row:two].astype(BF)

    def send_rows(j):
        rs.append(remote(rs_send.at[:, cols[j]], rs_recv.at[:, cols[j]], dev_b))

    def turn_d(src, dst, base):
        def head(h, carry):
            high = src[h]
            dst[h] = high.T
            delta[h, :, pl.ds(base, two)] = jnp.sum(
                high.astype(F32) * ot[h, :, pl.ds(base, two)].astype(F32), axis=0, keepdims=True
            )
            return carry

        lax.fori_loop(0, GROUP, head, 0)

    pass_near(0)
    pass_near(1)
    pass_own(2)
    loc_w.wait()
    loc_go.wait()
    go_b[0].wait_recv()
    cotangent(wm, dot_acc, 0)
    go_b[1].wait_recv()
    cotangent(wm, dot_acc, 1)
    pass_own(3)
    pass_far(0)
    pass_far(1)
    have(0)
    have(1)
    cotangent(wp, dot_acc_a, 0)
    cotangent(wp, dot_acc_a, 1)
    o_a.wait_recv()
    project(0)
    project(1)
    pass_near(2)
    go_b[2].wait_recv()
    cotangent(wm, dot_acc, 2)
    pass_near(3)
    go_b[3].wait_recv()
    send_rows(0)
    send_rows(1)
    cotangent(wm, dot_acc, 3)
    heads_of(dot_acc, dot_own)
    turn_d(dot_own, d_own, 0)
    pass_far(2)
    pass_far(3)
    have(2)
    have(3)
    cotangent(wp, dot_acc_a, 2)
    cotangent(wp, dot_acc_a, 3)
    heads_of(dot_acc_a, dot_send)
    d_a = remote(dot_send, dot_rem, dev_a)
    project(2)
    send_rows(2)
    project(3)
    send_rows(3)

    def backward(o, base, dt, dd, fresh):
        tl = pl.ds(base, two)

        def head(h, carry):
            s = dot(kb[o], qt[h, :, tl])
            p = jnp.exp2(s * c2 - (stat_l[h, :, tl] + bias[o]))
            if o == 0:
                at_u = lax.broadcasted_iota(jnp.int32, (tok, two), 0)
                p = jnp.where(at_u <= tabs_ref[:, tl], p, 0.0)
            dp = dot(vb[o], dt[h])
            ds = (p * (dp - delta[h, :, tl])).astype(BF)
            dv_acc[o] += dot(p.astype(BF), dd[h])
            dk_acc[o] += dot(ds, qh[h, tl])
            part_q = dot(kt[o], ds)
            if o == REACH - 1:
                dq_acc[h, :, tl] = part_q
            else:
                dq_acc[h, :, tl] += part_q
            return carry

        if fresh:
            dv_acc[o] = jnp.zeros((tok, HD), F32)
            dk_acc[o] = jnp.zeros((tok, HD), F32)
        lax.fori_loop(0, GROUP, head, 0)

    def own_rows(o):
        backward(o, 0, dot_own, d_own, True)

    def other_rows(o):
        backward(o, two, dot_rem, d_rem, False)

    back = []

    def send_back(o):
        gk, gv = dk_acc[o] * SCALE, dv_acc[o]
        if o < REACH - 1:
            back[-1].wait_recv()
            gk = gk + dkv_recv[o, :, 0:HD].astype(F32)
            gv = gv + dkv_recv[o, :, HD : 2 * HD].astype(F32)
        if o == 0:
            gk_out[...] = gk.astype(BF)
            gv_out[...] = gv.astype(BF)
        else:
            dkv_send[o - 1, :, 0:HD] = gk.astype(BF)
            dkv_send[o - 1, :, HD : 2 * HD] = gv.astype(BF)
            back.append(remote(dkv_send.at[o - 1], dkv_recv.at[o - 1], at(-1)))

    own_rows(3)
    own_rows(2)
    d_a.wait_recv()
    turn_d(dot_rem, d_rem, two)
    other_rows(3)
    send_back(3)
    other_rows(2)
    own_rows(1)
    send_back(2)
    other_rows(1)
    own_rows(0)
    send_back(1)
    other_rows(0)

    outs = []

    def put(src, dst):
        c = pltpu.make_async_copy(src, dst, out_sem.at[len(outs)])
        c.start()
        outs.append(c)

    for h in range(GROUP):
        gq_out[:, h * HD : (h + 1) * HD] = (dq_acc[h] * SCALE).T.astype(BF)
    for s in range(N_TP):
        rows = pl.ds(pl.multiple_of(perm[s] * row, row), row)
        put(gq_out.at[pl.ds(s * row, row)], gq_ref.at[rows])

    for c in rs:
        c.wait_recv()
    lo_out[...] = (lo_acc[...] + rs_recv[...].astype(F32)).astype(BF)
    put(lo_out, lo_ref)

    send_back(0)
    put(gk_out, gk_ref)
    put(gv_out, gv_ref)

    sent = [c for pair in kv[1:] for c in pair] + wa + go_b + [o_a, d_a] + rs + back
    for j in range(CHUNKS):
        sent += [up[j], down[j], far[j]] + sibs[j]
    for c in sent:
        c.wait_send()
    for c in outs:
        c.wait()


def settle(*refs):
    many = len(refs) // 3
    came, went, held, sems = refs[:many], refs[many : 2 * many], refs[2 * many : -1], refs[-1]
    loads = [pltpu.make_async_copy(came[i], held[i], sems.at[0, i]) for i in range(many)]
    stores = [pltpu.make_async_copy(held[i], went[i], sems.at[1, i]) for i in range(many)]
    for c in loads:
        c.start()
    for load, store in zip(loads, stores):
        load.wait()
        store.start()
    for c in stores:
        c.wait()


def on_device(n, lengths, queries, key_vectors, value_vectors, out_weight, grad_output):
    tok, width = queries.shape
    feat = out_weight.shape[1]
    row, two = tok // N_TP, tok // 2
    docs = lengths.shape[0]
    hbm = pl.BlockSpec(memory_space=pl.ANY)
    vm = pltpu.VMEM
    dma = pltpu.SemaphoreType.DMA
    flops = 2 * tok * width * feat * 2 + 7 * 2 * tok * tok * width * REACH
    found = pl.pallas_call(
        functools.partial(kernel, n, docs),
        out_shape=(
            jax.ShapeDtypeStruct((row, feat), BF),
            jax.ShapeDtypeStruct((tok, width), BF),
            jax.ShapeDtypeStruct((tok, HD), BF),
            jax.ShapeDtypeStruct((tok, HD), BF),
        ),
        in_specs=[pl.BlockSpec(memory_space=pltpu.SMEM)] + [hbm] * 5,
        out_specs=(hbm,) * 4,
        scratch_shapes=[
            vm((GROUP, tok, HD), BF),
            vm((GROUP, HD, tok), BF),
            vm((REACH, tok, HD), BF),
            vm((REACH, tok, HD), BF),
            vm((REACH, HD, tok), BF),
            vm((REACH, HD, tok), BF),
            vm((PARTS, width // PARTS, feat), BF),
            vm((PARTS, width // PARTS, feat), BF),
            vm((2, row, feat), BF),
            vm((GROUP, HD, tok), F32),
            vm((GROUP, 1, tok), F32),
            vm((GROUP, 1, tok), F32),
            vm((GROUP, HD, tok), BF),
            vm((tok, width), BF),
            vm((two, width), BF),
            vm((row, feat), BF),
            vm((row, feat), BF),
            vm((row, feat), F32),
            vm((row, feat), BF),
            vm((width, two), F32),
            vm((width, two), F32),
            vm((GROUP, HD, two), BF),
            vm((GROUP, HD, two), BF),
            vm((GROUP, HD, two), BF),
            vm((GROUP, two, HD), BF),
            vm((GROUP, two, HD), BF),
            vm((GROUP, 1, tok), F32),
            vm((REACH, tok, HD), F32),
            vm((REACH, tok, HD), F32),
            vm((GROUP, HD, tok), F32),
            vm((REACH - 1, tok, 2 * HD), BF),
            vm((REACH - 1, tok, 2 * HD), BF),
            vm((tok, width), BF),
            vm((tok, HD), BF),
            vm((tok, HD), BF),
            vm((1, tok), jnp.int32),
            dma((4 + N_TP * GROUP,)),
            dma((7,)),
            dma((64,)),
            dma((64,)),
        ],
        compiler_params=pltpu.CompilerParams(
            collective_id=0, has_side_effects=True, vmem_limit_bytes=56 * 1024 * 1024
        ),
        cost_estimate=pl.CostEstimate(flops=flops, bytes_accessed=1 << 24, transcendentals=1 << 23),
    )(
        lengths,
        queries,
        key_vectors,
        value_vectors,
        out_weight.reshape(PARTS, width // PARTS, feat),
        grad_output,
    )
    return pl.pallas_call(
        settle,
        out_shape=tuple(jax.ShapeDtypeStruct(a.shape, a.dtype) for a in found),
        in_specs=[hbm] * 4,
        out_specs=(hbm,) * 4,
        scratch_shapes=[vm(a.shape, a.dtype) for a in found] + [dma((2, 4))],
    )(*found)


def solution(mesh):
    return jax.shard_map(
        functools.partial(on_device, mesh.shape["attn"]),
        mesh=mesh,
        in_specs=(
            P(),
            P("attn", "tp"),
            P("attn", "tp"),
            P("attn", "tp"),
            P("tp", None),
            P(("attn", "tp"), None),
        ),
        out_specs=(P(("attn", "tp"), None), P("attn", "tp"), P("attn", "tp"), P("attn", "tp")),
        check_vma=False,
    )
```

```python
import functools

import jax
import jax.numpy as jnp
from jax import lax
from jax.experimental import pallas as pl
from jax.experimental.pallas import tpu as pltpu
from jax.sharding import PartitionSpec as P

HD = 128
REACH = 4
GROUP = 5
N_TP = 4
PARTS = 8
A_CHUNKS, B_CHUNKS = 4, 2
CHUNKS = A_CHUNKS + B_CHUNKS
Z = 8
NEGATIVE = -1e30
SCALE = HD ** (-0.5)
LOG2E = 1.4426950408889634
MESH = pl.DeviceIdType.MESH
BF, F32 = jnp.bfloat16, jnp.float32


def dot(a, b):
    return jnp.dot(a, b, preferred_element_type=F32)


def dot_nt(a, b):
    return lax.dot_general(a, b, (((1,), (1,)), ((), ())), preferred_element_type=F32)


def kernel(
    n,
    docs,
    len_ref,
    q_ref,
    k_ref,
    v_ref,
    w_ref,
    go_ref,
    lo_ref,
    gq_ref,
    gk_ref,
    gv_ref,
    qh,
    qt,
    kb,
    vb,
    kt,
    vt,
    wm,
    wp,
    go,
    acc,
    stat_m,
    stat_l,
    ot,
    o_all,
    op,
    rs_send,
    rs_recv,
    lo_acc,
    lo_out,
    dot_own,
    dot_part,
    dot_other,
    dot_send,
    dot_recv,
    dt,
    dd,
    delta,
    dk_acc,
    dv_acc,
    dq_acc,
    dkv_send,
    dkv_recv,
    gq_out,
    gk_out,
    gv_out,
    tabs_ref,
    loc_sem,
    out_sem,
    send_sem,
    recv_sem,
):
    tok, width = q_ref.shape
    row = tok // N_TP
    two = 2 * row
    feat = go_ref.shape[1]
    me, y = lax.axis_index("attn"), lax.axis_index("tp")
    step_x = n // 4
    core = lax.rem(me, 2)
    x = me // step_x
    y_a = y + 1 - 2 * lax.rem(y, 2)
    y_b = N_TP - 1 - y
    perm = [y, y_b, y_a, N_TP - 1 - y_a]

    def at(shift):
        return (lax.rem(me + shift + n, n), y)

    dev_a, dev_b = (me, y_a), (me, y_b)
    x_up, x_down = at(step_x), at(-step_x)
    z = lax.rem(me // 2, Z)
    z_up = (me + (lax.rem(z + 1, Z) - z) * 2, y)
    z_down = (me + (lax.rem(z + Z - 1, Z) - z) * 2, y)
    sib = (me + 1 - 2 * core, y)

    def part_of(shift):
        return lax.rem(x + shift + 4, 4) * 2 + core

    partners = [at(1), at(-1)] + [dev_a, dev_b, x_up, x_down]
    partners += [z_up, z_down]
    barrier = pltpu.get_barrier_semaphore()
    for dev in partners:
        pl.semaphore_signal(barrier, inc=1, device_id=dev, device_id_type=MESH)

    def local(i, src, dst):
        c = pltpu.make_async_copy(src, dst, loc_sem.at[i])
        c.start()
        return c

    loc_k = local(0, k_ref, kb.at[0])
    loc_v = local(1, v_ref, vb.at[0])
    loc_q = []
    for s in range(N_TP):
        rows = pl.ds(pl.multiple_of(perm[s] * row, row), row)
        for h in range(GROUP):
            loc_q.append(
                local(
                    2 + s * GROUP + h,
                    q_ref.at[rows, pl.ds(h * HD, HD)],
                    qh.at[h, pl.ds(s * row, row)],
                )
            )
    loc_go = local(2 + N_TP * GROUP, go_ref, go.at[0])
    loc_w = local(3 + N_TP * GROUP, w_ref, wm)

    pl.semaphore_wait(barrier, len(partners))

    used = [0]

    def remote(src, dst, dev):
        i = used[0]
        used[0] += 1
        c = pltpu.make_async_remote_copy(
            src_ref=src,
            dst_ref=dst,
            send_sem=send_sem.at[i],
            recv_sem=recv_sem.at[i],
            device_id=dev,
            device_id_type=MESH,
        )
        c.start()
        return c

    z_base = feat * 3 // 5
    wide = [z_base // A_CHUNKS] * A_CHUNKS + [(feat - z_base) // B_CHUNKS] * B_CHUNKS
    cols = [pl.ds(sum(wide[:j]), wide[j]) for j in range(CHUNKS)]
    side = [0] * A_CHUNKS + [1] * B_CHUNKS
    mine, from_down, from_up, from_far = [part_of(s) for s in (0, -1, 1, 2)]
    kv = [None, (remote(k_ref, kb.at[1], at(1)), remote(v_ref, vb.at[1], at(1)))]
    rows_of = [(dev_b, dev_a)[i] for i in side]
    wa, go_in = {}, {}

    def ask_weights(j):
        part = w_ref.at[mine, :, cols[j]]
        wa[j] = remote(part, wp.at[mine, :, cols[j]], dev_a)

    def ask_rows(j):
        go_in[j] = remote(go_ref.at[:, cols[j]], go.at[1, :, cols[j]], rows_of[j])

    z_wide = (feat - z_base) // Z

    def z_piece(ref, shift, low=0, many=PARTS // 2):
        first_col = pl.multiple_of(z_base + lax.rem(z + shift + Z, Z) * z_wide, z_wide)
        return ref.at[pl.ds(core * (PARTS // 2) + low, many), :, pl.ds(first_col, z_wide)]

    ask_weights(0)
    wb = remote(z_piece(w_ref, 0), z_piece(wp, 0), dev_b)
    ask_weights(1)
    ask_rows(0)
    ask_weights(2)
    ask_weights(3)
    ask_rows(1)
    ask_rows(4)
    ask_rows(2)
    ask_rows(5)
    ask_rows(3)

    z_sibs, z_ups, z_downs = [], [], []

    def z_share(piece):
        z_sibs.append(remote(piece, piece, sib))

    def z_first():
        wb.wait_recv()
        piece = z_piece(wp, 0)
        z_ups.append(remote(piece, piece, z_up))
        z_downs.append(remote(piece, piece, z_down))
        z_share(piece)

    def z_next(hop):
        last = hop == Z // 2 - 1
        z_ups[-1].wait_recv()
        piece = z_piece(wp, -hop)
        part = z_piece(wp, -hop, 0, PARTS // 4) if last else piece
        z_ups.append(remote(part, part, z_up))
        z_share(piece)
        z_downs[-1].wait_recv()
        piece = z_piece(wp, hop)
        part = z_piece(wp, hop, PARTS // 4, PARTS // 4) if last else piece
        z_downs.append(remote(part, part, z_down))
        z_share(piece)

    def z_last():
        z_ups[-1].wait_recv()
        z_share(z_piece(wp, Z // 2, 0, PARTS // 4))
        z_downs[-1].wait_recv()
        z_share(z_piece(wp, Z // 2, PARTS // 4, PARTS // 4))

    up, down, far = {}, {}, {}
    sibs = [[] for _ in range(A_CHUNKS)]

    def pass_own(j):
        wa[j].wait_recv()
        piece = wp.at[mine, :, cols[j]]
        up[j] = remote(piece, piece, x_up)
        down[j] = remote(piece, piece, x_down)
        sibs[j].append(remote(piece, piece, sib))

    def pass_near(j):
        up[j].wait_recv()
        piece = wp.at[from_down, :, cols[j]]
        if j % 2 == 0:
            far[j] = remote(piece, piece, x_up)
        sibs[j].append(remote(piece, piece, sib))
        down[j].wait_recv()
        piece = wp.at[from_up, :, cols[j]]
        if j % 2 == 1:
            far[j] = remote(piece, piece, x_down)
        sibs[j].append(remote(piece, piece, sib))

    def pass_far(j):
        far[j].wait_recv()
        piece = wp.at[from_far, :, cols[j]]
        sibs[j].append(remote(piece, piece, sib))

    def have(j):
        for c in sibs[j]:
            c.wait_recv()

    def next_keys(o):
        for c in kv[o]:
            c.wait_recv()
        if o < REACH - 1:
            kv.append(
                (
                    remote(kb.at[o], kb.at[o + 1], at(1)),
                    remote(vb.at[o], vb.at[o + 1], at(1)),
                )
            )

    end, first = jnp.int32(0), jnp.int32(0)
    for d in range(docs):
        end = end + len_ref[d]
        first = jnp.where(end <= me, end, first)
    depth = me - first
    bias = [jnp.where(o <= depth, 0.0, -NEGATIVE).astype(F32) for o in range(REACH)]

    lane = lax.broadcasted_iota(jnp.int32, (1, row), 1)
    for s in range(N_TP):
        tabs_ref[:, s * row : (s + 1) * row] = lane + perm[s] * row

    c2 = SCALE * LOG2E

    for c in loc_q:
        c.wait()

    def turn_q(h, carry):
        qt[h] = qh[h].T
        return carry

    lax.fori_loop(0, GROUP, turn_q, 0)

    def turn_kv(o):
        kt[o] = kb[o].T
        vt[o] = vb[o].T

    def forward(o):
        turn_kv(o)

        def head(h, carry):
            s = dot(kb[o], qt[h])
            if o == 0:
                at_u = lax.broadcasted_iota(jnp.int32, (tok, tok), 0)
                s = jnp.where(at_u <= tabs_ref[...], s, NEGATIVE)
                new = jnp.max(s, axis=0, keepdims=True)
                p = jnp.exp2((s - new) * c2)
                stat_l[h] = jnp.sum(p, axis=0, keepdims=True)
                acc[h] = dot(vt[o], p.astype(BF))
            else:
                old = stat_m[h]
                new = jnp.maximum(old, jnp.max(s, axis=0, keepdims=True) - bias[o])
                fade = jnp.exp2((old - new) * c2)
                p = jnp.exp2((s - (new + bias[o])) * c2)
                stat_l[h] = stat_l[h] * fade + jnp.sum(p, axis=0, keepdims=True)
                acc[h] = acc[h] * fade + dot(vt[o], p.astype(BF))
            stat_m[h] = new

        for h in range(GROUP):
            head(h, None)

    loc_k.wait()
    loc_v.wait()
    forward(0)
    next_keys(1)
    z_first()
    pass_own(0)
    forward(1)
    pass_own(1)
    next_keys(2)
    forward(2)
    pass_own(2)
    z_next(1)
    next_keys(3)
    forward(3)
    pass_own(3)

    for h in range(GROUP):
        low = (acc[h] * (1.0 / stat_l[h])).astype(BF)
        ot[h] = low
        o_all[:, h * HD : (h + 1) * HD] = low.T
        stat_l[h] = stat_m[h] * c2 + jnp.log2(stat_l[h])
    o_in = [
        remote(o_all.at[pl.ds(two, two)], op.at[0], dev_a),
        remote(o_all.at[pl.ds(row, row)], op.at[1, pl.ds(0, row)], dev_b),
        remote(o_all.at[pl.ds(3 * row, row)], op.at[1, pl.ds(row, row)], dev_b),
    ]
    def weights(w3, j):
        return w3[:, :, cols[j]].reshape(width, wide[j])

    def add_to(total, part, fresh):
        if fresh:
            total[...] = part
        else:
            total[...] += part

    def cotangent_own():
        for j in range(CHUNKS):
            add_to(dot_own, dot_nt(weights(wm, j), go[0, :, cols[j]]), j == 0)

    def cotangent_rows(j):
        fresh = j in (0, A_CHUNKS)
        add_to(dot_part.at[side[j]], dot_nt(weights(wm, j), go[1, :, cols[j]]), fresh)

    def cotangent_other(j):
        both = go[:, :, cols[j]].reshape(two, wide[j])
        add_to(dot_other.at[side[j]], dot_nt(weights(wp, j), both), j in (0, A_CHUNKS))

    def send_cotangent(i):
        for h in range(GROUP):
            dot_send[i, h] = dot_other[i, h * HD : (h + 1) * HD, :].astype(BF)
        return remote(dot_send.at[i], dot_recv.at[i], [dev_a, dev_b][i])

    rs = {}

    def project(j):
        if side[j] == 0:
            mine_o, other_o = o_all[0:two], op[0]
        else:
            mine_o = jnp.concatenate([o_all[0:row], o_all[two : two + row]], axis=0)
            other_o = op[1]
        one = dot(mine_o, weights(wm, j)).astype(BF)
        other = dot(other_o, weights(wp, j)).astype(BF)
        both = one.astype(F32) + other.astype(F32)
        lo_acc[:, cols[j]] = both[0:row]
        rs_send[:, cols[j]] = both[row:two].astype(BF)

    def send_rows(j):
        rs[j] = remote(rs_send.at[:, cols[j]], rs_recv.at[:, cols[j]], rows_of[j])

    def turn_d(h, base, size, high):
        dt[h, :, base : base + size] = high
        dd[h, base : base + size] = high.T
        delta[h, :, base : base + size] = jnp.sum(
            high.astype(F32) * ot[h, :, base : base + size].astype(F32), axis=0, keepdims=True
        )

    def turn_own():
        for h in range(GROUP):
            turn_d(h, 0, row, dot_own[h * HD : (h + 1) * HD, :].astype(BF))

    def turn_rest():
        for h in range(GROUP):
            at_h = slice(h * HD, (h + 1) * HD)
            from_a, from_b = dot_recv[0, h].astype(F32), dot_recv[1, h].astype(F32)
            turn_d(h, row, row, (dot_part[0, at_h] + from_b[:, 0:row]).astype(BF))
            turn_d(h, two, row, (dot_part[1, at_h] + from_a[:, 0:row]).astype(BF))
            turn_d(h, 3 * row, row, (from_a[:, row:two] + from_b[:, row:two]).astype(BF))

    def backward(o, base, size):
        tl = slice(base, base + size)

        def head(h, carry):
            s = dot(kb[o], qt[h, :, tl])
            p = jnp.exp2(s * c2 - (stat_l[h, :, tl] + bias[o]))
            if o == 0:
                at_u = lax.broadcasted_iota(jnp.int32, (tok, size), 0)
                p = jnp.where(at_u <= tabs_ref[:, tl], p, 0.0)
            dp = dot(vb[o], dt[h, :, tl])
            ds = (p * (dp - delta[h, :, tl])).astype(BF)
            part_v, part_k = dot(p.astype(BF), dd[h, tl]), dot(ds, qh[h, tl])
            if base == 0 and h == 0:
                dv_acc[o] = part_v
                dk_acc[o] = part_k
            else:
                dv_acc[o] += part_v
                dk_acc[o] += part_k
            part_q = dot(kt[o], ds)
            if o == REACH - 1:
                dq_acc[h, :, tl] = part_q
            else:
                dq_acc[h, :, tl] += part_q

        for h in range(GROUP):
            head(h, None)

    def own_rows(o):
        backward(o, 0, row)

    def other_rows(o):
        backward(o, row, tok - row)

    pass_near(0)
    pass_near(1)
    loc_w.wait()
    loc_go.wait()
    cotangent_own()
    turn_own()
    z_next(2)
    own_rows(3)
    pass_near(2)
    pass_near(3)
    for j in (0, 1):
        go_in[j].wait_recv()
        cotangent_rows(j)
    own_rows(2)
    z_next(3)
    for j in (2, 3, 4, 5):
        go_in[j].wait_recv()
        cotangent_rows(j)
    for j in range(A_CHUNKS):
        pass_far(j)
    z_last()
    for j in range(A_CHUNKS):
        have(j)
        cotangent_other(j)
    d_in = [send_cotangent(0)]
    for c in z_sibs:
        c.wait_recv()
    cotangent_other(4)
    cotangent_other(5)
    d_in.append(send_cotangent(1))
    o_in[0].wait_recv()
    for j in (0, 1):
        project(j)
        send_rows(j)
    o_in[1].wait_recv()
    o_in[2].wait_recv()
    for j in (4, 2, 5, 3):
        project(j)
        send_rows(j)
    own_rows(1)
    own_rows(0)
    for c in d_in:
        c.wait_recv()
    turn_rest()

    back = []

    def send_back(o):
        gk, gv = dk_acc[o] * SCALE, dv_acc[o]
        if o < REACH - 1:
            back[-1].wait_recv()
            gk = gk + dkv_recv[o, :, 0:HD].astype(F32)
            gv = gv + dkv_recv[o, :, HD : 2 * HD].astype(F32)
        if o == 0:
            gk_out[...] = gk.astype(BF)
            gv_out[...] = gv.astype(BF)
        else:
            dkv_send[o - 1, :, 0:HD] = gk.astype(BF)
            dkv_send[o - 1, :, HD : 2 * HD] = gv.astype(BF)
            back.append(remote(dkv_send.at[o - 1], dkv_recv.at[o - 1], at(-1)))

    for o in range(REACH - 1, 0, -1):
        other_rows(o)
        send_back(o)
    other_rows(0)

    outs = []

    def put(src, dst):
        c = pltpu.make_async_copy(src, dst, out_sem.at[len(outs)])
        c.start()
        outs.append(c)

    for h in range(GROUP):
        gq_out[:, h * HD : (h + 1) * HD] = (dq_acc[h] * SCALE).T.astype(BF)
    for s in range(N_TP):
        rows = pl.ds(pl.multiple_of(perm[s] * row, row), row)
        put(gq_out.at[pl.ds(s * row, row)], gq_ref.at[rows])

    for j in range(CHUNKS):
        rs[j].wait_recv()
        lo_out[:, cols[j]] = (lo_acc[:, cols[j]] + rs_recv[:, cols[j]].astype(F32)).astype(BF)
        put(lo_out.at[:, cols[j]], lo_ref.at[:, cols[j]])

    send_back(0)
    put(gk_out, gk_ref)
    put(gv_out, gv_ref)

    sent = [c for pair in kv[1:] for c in pair] + o_in + d_in + back
    sent += [wb] + z_sibs + z_ups + z_downs
    for j in range(CHUNKS):
        sent += [go_in[j], rs[j]]
    for j in range(A_CHUNKS):
        sent += [wa[j], up[j], down[j], far[j]] + sibs[j]
    for c in sent:
        c.wait_send()
    for c in outs:
        c.wait()


def settle(*refs):
    many = len(refs) // 3
    came, went, held, sems = refs[:many], refs[many : 2 * many], refs[2 * many : -1], refs[-1]
    loads = [pltpu.make_async_copy(came[i], held[i], sems.at[0, i]) for i in range(many)]
    stores = [pltpu.make_async_copy(held[i], went[i], sems.at[1, i]) for i in range(many)]
    for c in loads:
        c.start()
    for load, store in zip(loads, stores):
        load.wait()
        store.start()
    for c in stores:
        c.wait()


def on_device(n, lengths, queries, key_vectors, value_vectors, out_weight, grad_output):
    tok, width = queries.shape
    feat = out_weight.shape[1]
    row, two = tok // N_TP, tok // 2
    docs = lengths.shape[0]
    hbm = pl.BlockSpec(memory_space=pl.ANY)
    vm = pltpu.VMEM
    dma = pltpu.SemaphoreType.DMA
    flops = 2 * tok * width * feat * 2 + 7 * 2 * tok * tok * width * REACH
    found = pl.pallas_call(
        functools.partial(kernel, n, docs),
        out_shape=(
            jax.ShapeDtypeStruct((row, feat), BF),
            jax.ShapeDtypeStruct((tok, width), BF),
            jax.ShapeDtypeStruct((tok, HD), BF),
            jax.ShapeDtypeStruct((tok, HD), BF),
        ),
        in_specs=[pl.BlockSpec(memory_space=pltpu.SMEM)] + [hbm] * 5,
        out_specs=(hbm,) * 4,
        scratch_shapes=[
            vm((GROUP, tok, HD), BF),
            vm((GROUP, HD, tok), BF),
            vm((REACH, tok, HD), BF),
            vm((REACH, tok, HD), BF),
            vm((REACH, HD, tok), BF),
            vm((REACH, HD, tok), BF),
            vm((PARTS, width // PARTS, feat), BF),
            vm((PARTS, width // PARTS, feat), BF),
            vm((2, row, feat), BF),
            vm((GROUP, HD, tok), F32),
            vm((GROUP, 1, tok), F32),
            vm((GROUP, 1, tok), F32),
            vm((GROUP, HD, tok), BF),
            vm((tok, width), BF),
            vm((2, two, width), BF),
            vm((row, feat), BF),
            vm((row, feat), BF),
            vm((row, feat), F32),
            vm((row, feat), BF),
            vm((width, row), F32),
            vm((2, width, row), F32),
            vm((2, width, two), F32),
            vm((2, GROUP, HD, two), BF),
            vm((2, GROUP, HD, two), BF),
            vm((GROUP, HD, tok), BF),
            vm((GROUP, tok, HD), BF),
            vm((GROUP, 1, tok), F32),
            vm((REACH, tok, HD), F32),
            vm((REACH, tok, HD), F32),
            vm((GROUP, HD, tok), F32),
            vm((REACH - 1, tok, 2 * HD), BF),
            vm((REACH - 1, tok, 2 * HD), BF),
            vm((tok, width), BF),
            vm((tok, HD), BF),
            vm((tok, HD), BF),
            vm((1, tok), jnp.int32),
            dma((4 + N_TP * GROUP,)),
            dma((16,)),
            dma((96,)),
            dma((96,)),
        ],
        compiler_params=pltpu.CompilerParams(
            collective_id=0, has_side_effects=True, vmem_limit_bytes=56 * 1024 * 1024
        ),
        cost_estimate=pl.CostEstimate(flops=flops, bytes_accessed=1 << 24, transcendentals=1 << 23),
    )(
        lengths,
        queries,
        key_vectors,
        value_vectors,
        out_weight.reshape(PARTS, width // PARTS, feat),
        grad_output,
    )
    return pl.pallas_call(
        settle,
        out_shape=tuple(jax.ShapeDtypeStruct(a.shape, a.dtype) for a in found),
        in_specs=[hbm] * 4,
        out_specs=(hbm,) * 4,
        scratch_shapes=[vm(a.shape, a.dtype) for a in found] + [dma((2, 4))],
    )(*found)


def solution(mesh):
    return jax.shard_map(
        functools.partial(on_device, mesh.shape["attn"]),
        mesh=mesh,
        in_specs=(
            P(),
            P("attn", "tp"),
            P("attn", "tp"),
            P("attn", "tp"),
            P("tp", None),
            P(("attn", "tp"), None),
        ),
        out_specs=(P(("attn", "tp"), None), P("attn", "tp"), P("attn", "tp"), P("attn", "tp")),
        check_vma=False,
    )
```

```python
import functools

import jax
import jax.numpy as jnp
from jax import lax
from jax.experimental import pallas as pl
from jax.experimental.pallas import tpu as pltpu
from jax.sharding import PartitionSpec as P

HD = 128
REACH = 4
GROUP = 5
N_TP = 4
PARTS = 8
A_CHUNKS, B_CHUNKS = 4, 2
CHUNKS = A_CHUNKS + B_CHUNKS
Z = 8
NEGATIVE = -1e30
SCALE = HD ** (-0.5)
LOG2E = 1.4426950408889634
MESH = pl.DeviceIdType.MESH
BF, F32 = jnp.bfloat16, jnp.float32


def dot(a, b):
    return jnp.dot(a, b, preferred_element_type=F32)


def dot_nt(a, b):
    return lax.dot_general(a, b, (((1,), (1,)), ((), ())), preferred_element_type=F32)


def kernel(
    n,
    docs,
    len_ref,
    q_ref,
    k_ref,
    v_ref,
    w_ref,
    go_ref,
    lo_ref,
    gq_ref,
    gk_ref,
    gv_ref,
    qh,
    qt,
    kb,
    vb,
    kt,
    vt,
    wm,
    wp,
    go,
    acc,
    stat_m,
    stat_l,
    ot,
    o_all,
    op,
    rs_send,
    rs_recv,
    lo_acc,
    lo_out,
    dot_own,
    dot_part,
    dot_other,
    dot_send,
    dot_recv,
    dt,
    dd,
    delta,
    dk_acc,
    dv_acc,
    dq_acc,
    dkv_send,
    dkv_recv,
    gq_out,
    gk_out,
    gv_out,
    tabs_ref,
    loc_sem,
    out_sem,
    send_sem,
    recv_sem,
):
    tok, width = q_ref.shape
    row = tok // N_TP
    two = 2 * row
    feat = go_ref.shape[1]
    me, y = lax.axis_index("attn"), lax.axis_index("tp")
    step_x = n // 4
    core = lax.rem(me, 2)
    x = me // step_x
    y_a = y + 1 - 2 * lax.rem(y, 2)
    y_b = N_TP - 1 - y
    perm = [y, y_b, y_a, N_TP - 1 - y_a]

    def at(shift):
        return (lax.rem(me + shift + n, n), y)

    dev_a, dev_b = (me, y_a), (me, y_b)
    x_up, x_down = at(step_x), at(-step_x)
    z = lax.rem(me // 2, Z)
    z_up = (me + (lax.rem(z + 1, Z) - z) * 2, y)
    z_down = (me + (lax.rem(z + Z - 1, Z) - z) * 2, y)
    sib = (me + 1 - 2 * core, y)

    def part_of(shift):
        return lax.rem(x + shift + 4, 4) * 2 + core

    partners = [at(1), at(-1)] + [dev_a, dev_b, x_up, x_down]
    partners += [z_up, z_down]
    barrier = pltpu.get_barrier_semaphore()
    for dev in partners:
        pl.semaphore_signal(barrier, inc=1, device_id=dev, device_id_type=MESH)

    def local(i, src, dst):
        c = pltpu.make_async_copy(src, dst, loc_sem.at[i])
        c.start()
        return c

    loc_k = local(0, k_ref, kb.at[0])
    loc_v = local(1, v_ref, vb.at[0])
    loc_q = []
    for s in range(N_TP):
        rows = pl.ds(pl.multiple_of(perm[s] * row, row), row)
        for h in range(GROUP):
            loc_q.append(
                local(
                    2 + s * GROUP + h,
                    q_ref.at[rows, pl.ds(h * HD, HD)],
                    qh.at[h, pl.ds(s * row, row)],
                )
            )
    loc_go = local(2 + N_TP * GROUP, go_ref, go.at[0])
    loc_w = local(3 + N_TP * GROUP, w_ref, wm)

    pl.semaphore_wait(barrier, len(partners))

    used = [0]

    def remote(src, dst, dev):
        i = used[0]
        used[0] += 1
        c = pltpu.make_async_remote_copy(
            src_ref=src,
            dst_ref=dst,
            send_sem=send_sem.at[i],
            recv_sem=recv_sem.at[i],
            device_id=dev,
            device_id_type=MESH,
        )
        c.start()
        return c

    z_base = feat * 3 // 5
    wide = [z_base // A_CHUNKS] * A_CHUNKS + [(feat - z_base) // B_CHUNKS] * B_CHUNKS
    cols = [pl.ds(sum(wide[:j]), wide[j]) for j in range(CHUNKS)]
    side = [0] * A_CHUNKS + [1] * B_CHUNKS
    mine, from_down, from_up, from_far = [part_of(s) for s in (0, -1, 1, 2)]
    kv = [None, (remote(k_ref, kb.at[1], at(1)), remote(v_ref, vb.at[1], at(1)))]
    rows_of = [(dev_b, dev_a)[i] for i in side]
    wa, go_in = {}, {}

    def ask_weights(j):
        part = w_ref.at[mine, :, cols[j]]
        wa[j] = remote(part, wp.at[mine, :, cols[j]], dev_a)

    def ask_rows(j):
        go_in[j] = remote(go_ref.at[:, cols[j]], go.at[1, :, cols[j]], rows_of[j])

    z_wide = (feat - z_base) // Z

    def z_piece(ref, shift, low=0, many=PARTS // 2):
        first_col = pl.multiple_of(z_base + lax.rem(z + shift + Z, Z) * z_wide, z_wide)
        return ref.at[pl.ds(core * (PARTS // 2) + low, many), :, pl.ds(first_col, z_wide)]

    ask_weights(0)
    wb = remote(z_piece(w_ref, 0), z_piece(wp, 0), dev_b)
    ask_weights(1)
    ask_rows(0)
    ask_weights(2)
    ask_weights(3)
    ask_rows(1)
    ask_rows(4)
    ask_rows(2)
    ask_rows(5)
    ask_rows(3)

    z_sibs, z_ups, z_downs = [], [], []

    def z_share(piece):
        z_sibs.append(remote(piece, piece, sib))

    def z_first():
        wb.wait_recv()
        piece = z_piece(wp, 0)
        z_ups.append(remote(piece, piece, z_up))
        z_downs.append(remote(piece, piece, z_down))
        z_share(piece)

    def z_next(hop):
        last = hop == Z // 2 - 1
        z_ups[-1].wait_recv()
        piece = z_piece(wp, -hop)
        part = z_piece(wp, -hop, 0, PARTS // 4) if last else piece
        z_ups.append(remote(part, part, z_up))
        z_share(piece)
        z_downs[-1].wait_recv()
        piece = z_piece(wp, hop)
        part = z_piece(wp, hop, PARTS // 4, PARTS // 4) if last else piece
        z_downs.append(remote(part, part, z_down))
        z_share(piece)

    def z_last():
        z_ups[-1].wait_recv()
        z_share(z_piece(wp, Z // 2, 0, PARTS // 4))
        z_downs[-1].wait_recv()
        z_share(z_piece(wp, Z // 2, PARTS // 4, PARTS // 4))

    up, down, far = {}, {}, {}
    sibs = [[] for _ in range(A_CHUNKS)]

    def pass_own(j):
        wa[j].wait_recv()
        piece = wp.at[mine, :, cols[j]]
        up[j] = remote(piece, piece, x_up)
        down[j] = remote(piece, piece, x_down)
        sibs[j].append(remote(piece, piece, sib))

    def pass_near(j):
        up[j].wait_recv()
        piece = wp.at[from_down, :, cols[j]]
        if j % 2 == 0:
            far[j] = remote(piece, piece, x_up)
        sibs[j].append(remote(piece, piece, sib))
        down[j].wait_recv()
        piece = wp.at[from_up, :, cols[j]]
        if j % 2 == 1:
            far[j] = remote(piece, piece, x_down)
        sibs[j].append(remote(piece, piece, sib))

    def pass_far(j):
        far[j].wait_recv()
        piece = wp.at[from_far, :, cols[j]]
        sibs[j].append(remote(piece, piece, sib))

    def have(j):
        for c in sibs[j]:
            c.wait_recv()

    def next_keys(o):
        for c in kv[o]:
            c.wait_recv()
        if o < REACH - 1:
            kv.append(
                (
                    remote(kb.at[o], kb.at[o + 1], at(1)),
                    remote(vb.at[o], vb.at[o + 1], at(1)),
                )
            )

    end, first = jnp.int32(0), jnp.int32(0)
    for d in range(docs):
        end = end + len_ref[d]
        first = jnp.where(end <= me, end, first)
    depth = me - first

    def bias(o):
        return jnp.where(o <= depth, 0.0, -NEGATIVE).astype(F32)


    lane = lax.broadcasted_iota(jnp.int32, (1, row), 1)
    for s in range(N_TP):
        tabs_ref[:, s * row : (s + 1) * row] = lane + perm[s] * row

    c2 = SCALE * LOG2E

    for c in loc_q:
        c.wait()

    def turn_q(h, carry):
        qt[h] = qh[h].T
        return carry

    lax.fori_loop(0, GROUP, turn_q, 0)

    def turn_kv(o):
        kt[o] = kb[o].T
        vt[o] = vb[o].T

    def forward(o):
        turn_kv(o)

        def head(h, carry):
            s = dot(kb[o], qt[h])
            if o == 0:
                at_u = lax.broadcasted_iota(jnp.int32, (tok, tok), 0)
                s = jnp.where(at_u <= tabs_ref[...], s, NEGATIVE)
                new = jnp.max(s, axis=0, keepdims=True)
                p = jnp.exp2((s - new) * c2)
                stat_l[h] = jnp.sum(p, axis=0, keepdims=True)
                acc[h] = dot(vt[o], p.astype(BF))
            else:
                old = stat_m[h]
                new = jnp.maximum(old, jnp.max(s, axis=0, keepdims=True) - bias(o))
                fade = jnp.exp2((old - new) * c2)
                p = jnp.exp2((s - (new + bias(o))) * c2)
                stat_l[h] = stat_l[h] * fade + jnp.sum(p, axis=0, keepdims=True)
                acc[h] = acc[h] * fade + dot(vt[o], p.astype(BF))
            stat_m[h] = new

        for h in range(GROUP):
            head(h, None)

    loc_k.wait()
    loc_v.wait()
    forward(0)
    next_keys(1)
    z_first()
    pass_own(0)
    forward(1)
    pass_own(1)
    next_keys(2)
    forward(2)
    pass_own(2)
    z_next(1)
    next_keys(3)
    forward(3)
    pass_own(3)

    for h in range(GROUP):
        low = (acc[h] * (1.0 / stat_l[h])).astype(BF)
        ot[h] = low
        o_all[:, h * HD : (h + 1) * HD] = low.T
        stat_l[h] = stat_m[h] * c2 + jnp.log2(stat_l[h])
    o_in = [
        remote(o_all.at[pl.ds(two, two)], op.at[0], dev_a),
        remote(o_all.at[pl.ds(row, row)], op.at[1, pl.ds(0, row)], dev_b),
        remote(o_all.at[pl.ds(3 * row, row)], op.at[1, pl.ds(row, row)], dev_b),
    ]
    def weights(w3, j):
        return w3[:, :, cols[j]].reshape(width, wide[j])

    def add_to(total, part, fresh):
        if fresh:
            total[...] = part
        else:
            total[...] += part

    def cotangent_own():
        for j in range(CHUNKS):
            add_to(dot_own, dot_nt(weights(wm, j), go[0, :, cols[j]]), j == 0)

    def cotangent_rows(j):
        fresh = j in (0, A_CHUNKS)
        add_to(dot_part.at[side[j]], dot_nt(weights(wm, j), go[1, :, cols[j]]), fresh)

    def cotangent_other(j):
        both = go[:, :, cols[j]].reshape(two, wide[j])
        add_to(dot_other.at[side[j]], dot_nt(weights(wp, j), both), j in (0, A_CHUNKS))

    def send_cotangent(i):
        for h in range(GROUP):
            dot_send[i, h] = dot_other[i, h * HD : (h + 1) * HD, :].astype(BF)
        return remote(dot_send.at[i], dot_recv.at[i], [dev_a, dev_b][i])

    rs = {}

    def project(j):
        if side[j] == 0:
            mine_o, other_o = o_all[0:two], op[0]
        else:
            mine_o = jnp.concatenate([o_all[0:row], o_all[two : two + row]], axis=0)
            other_o = op[1]
        one = dot(mine_o, weights(wm, j)).astype(BF)
        other = dot(other_o, weights(wp, j)).astype(BF)
        both = one.astype(F32) + other.astype(F32)
        lo_acc[:, cols[j]] = both[0:row]
        rs_send[:, cols[j]] = both[row:two].astype(BF)

    def send_rows(j):
        rs[j] = remote(rs_send.at[:, cols[j]], rs_recv.at[:, cols[j]], rows_of[j])

    def turn_d(h, base, size, high):
        dt[h, :, base : base + size] = high
        dd[h, base : base + size] = high.T
        delta[h, :, base : base + size] = jnp.sum(
            high.astype(F32) * ot[h, :, base : base + size].astype(F32), axis=0, keepdims=True
        )

    def turn_own():
        for h in range(GROUP):
            turn_d(h, 0, row, dot_own[h * HD : (h + 1) * HD, :].astype(BF))

    def turn_rest():
        for h in range(GROUP):
            at_h = slice(h * HD, (h + 1) * HD)
            from_a, from_b = dot_recv[0, h].astype(F32), dot_recv[1, h].astype(F32)
            turn_d(h, row, row, (dot_part[0, at_h] + from_b[:, 0:row]).astype(BF))
            turn_d(h, two, row, (dot_part[1, at_h] + from_a[:, 0:row]).astype(BF))
            turn_d(h, 3 * row, row, (from_a[:, row:two] + from_b[:, row:two]).astype(BF))

    def backward(o, base, size):
        tl = slice(base, base + size)
        out = bias(o)

        def head(h):
            s = dot(kb[o], qt[h, :, tl])
            p = jnp.exp2(s * c2 - (stat_l[h, :, tl] + out))
            if base == 0 or (isinstance(o, int) and o == 0):
                at_u = lax.broadcasted_iota(jnp.int32, (tok, size), 0)
                p = jnp.where(at_u <= tabs_ref[:, tl] + jnp.where(o > 0, tok, 0), p, 0.0)
            dp = dot(vb[o], dt[h, :, tl])
            ds = (p * (dp - delta[h, :, tl])).astype(BF)
            part_v, part_k = dot(p.astype(BF), dd[h, tl]), dot(ds, qh[h, tl])
            if base == 0 and h == 0:
                dv_acc[o] = part_v
                dk_acc[o] = part_k
            else:
                dv_acc[o] += part_v
                dk_acc[o] += part_k
            dq_acc[h, :, tl] += dot(kt[o], ds)

        for h in range(GROUP):
            head(h)

    def own_rows(i, carry):
        backward(REACH - 1 - i, 0, row)
        return carry

    dq_acc[...] = jnp.zeros_like(dq_acc)
    dkv_recv[REACH - 1] = jnp.zeros((tok, 2 * HD), BF)

    pass_near(0)
    pass_near(1)
    loc_w.wait()
    loc_go.wait()
    cotangent_own()
    turn_own()
    z_next(2)
    lax.fori_loop(0, 2, own_rows, 0)
    pass_near(2)
    pass_near(3)
    for j in (0, 1):
        go_in[j].wait_recv()
        cotangent_rows(j)
    z_next(3)
    for j in (2, 3, 4, 5):
        go_in[j].wait_recv()
        cotangent_rows(j)
    for j in range(A_CHUNKS):
        pass_far(j)
    z_last()
    for j in range(A_CHUNKS):
        have(j)
        cotangent_other(j)
    d_in = [send_cotangent(0)]
    for c in z_sibs:
        c.wait_recv()
    cotangent_other(4)
    cotangent_other(5)
    d_in.append(send_cotangent(1))
    o_in[0].wait_recv()
    for j in (0, 1):
        project(j)
        send_rows(j)
    o_in[1].wait_recv()
    o_in[2].wait_recv()
    for j in (4, 2, 5, 3):
        project(j)
        send_rows(j)
    lax.fori_loop(2, REACH, own_rows, 0)
    for c in d_in:
        c.wait_recv()
    turn_rest()

    back_at = used[0]

    def back_copy(o):
        i = back_at + o
        c = pltpu.make_async_remote_copy(
            src_ref=dkv_send.at[o - 1],
            dst_ref=dkv_recv.at[o - 1],
            send_sem=send_sem.at[i],
            recv_sem=recv_sem.at[i],
            device_id=at(-1),
            device_id_type=MESH,
        )
        return c

    def sums(o):
        gk = dk_acc[o] * SCALE + dkv_recv[o, :, 0:HD].astype(F32)
        gv = dv_acc[o] + dkv_recv[o, :, HD : 2 * HD].astype(F32)
        return gk.astype(BF), gv.astype(BF)

    def other_rows(i, carry):
        o = REACH - 1 - i
        backward(o, row, tok - row)

        @pl.when(o < REACH - 1)
        def _():
            back_copy(o + 1).wait_recv()

        gk, gv = sums(o)
        dkv_send[o - 1, :, 0:HD] = gk
        dkv_send[o - 1, :, HD : 2 * HD] = gv
        back_copy(o).start()
        return carry

    lax.fori_loop(0, REACH - 1, other_rows, 0)
    backward(0, row, tok - row)

    outs = []

    def put(src, dst):
        c = pltpu.make_async_copy(src, dst, out_sem.at[len(outs)])
        c.start()
        outs.append(c)

    for h in range(GROUP):
        gq_out[:, h * HD : (h + 1) * HD] = (dq_acc[h] * SCALE).T.astype(BF)
    for s in range(N_TP):
        rows = pl.ds(pl.multiple_of(perm[s] * row, row), row)
        put(gq_out.at[pl.ds(s * row, row)], gq_ref.at[rows])

    for j in range(CHUNKS):
        rs[j].wait_recv()
        lo_out[:, cols[j]] = (lo_acc[:, cols[j]] + rs_recv[:, cols[j]].astype(F32)).astype(BF)
        put(lo_out.at[:, cols[j]], lo_ref.at[:, cols[j]])

    back_copy(1).wait_recv()
    gk_out[...], gv_out[...] = sums(0)
    put(gk_out, gk_ref)
    put(gv_out, gv_ref)

    sent = [c for pair in kv[1:] for c in pair] + o_in + d_in
    sent += [back_copy(o) for o in range(1, REACH)]
    sent += [wb] + z_sibs + z_ups + z_downs
    for j in range(CHUNKS):
        sent += [go_in[j], rs[j]]
    for j in range(A_CHUNKS):
        sent += [wa[j], up[j], down[j], far[j]] + sibs[j]
    for c in sent:
        c.wait_send()
    for c in outs:
        c.wait()


def settle(*refs):
    many = len(refs) // 3
    came, went, held, sems = refs[:many], refs[many : 2 * many], refs[2 * many : -1], refs[-1]
    loads = [pltpu.make_async_copy(came[i], held[i], sems.at[0, i]) for i in range(many)]
    stores = [pltpu.make_async_copy(held[i], went[i], sems.at[1, i]) for i in range(many)]
    for c in loads:
        c.start()
    for load, store in zip(loads, stores):
        load.wait()
        store.start()
    for c in stores:
        c.wait()


def on_device(n, lengths, queries, key_vectors, value_vectors, out_weight, grad_output):
    tok, width = queries.shape
    feat = out_weight.shape[1]
    row, two = tok // N_TP, tok // 2
    docs = lengths.shape[0]
    hbm = pl.BlockSpec(memory_space=pl.ANY)
    vm = pltpu.VMEM
    dma = pltpu.SemaphoreType.DMA
    flops = 2 * tok * width * feat * 2 + 7 * 2 * tok * tok * width * REACH
    found = pl.pallas_call(
        functools.partial(kernel, n, docs),
        out_shape=(
            jax.ShapeDtypeStruct((row, feat), BF),
            jax.ShapeDtypeStruct((tok, width), BF),
            jax.ShapeDtypeStruct((tok, HD), BF),
            jax.ShapeDtypeStruct((tok, HD), BF),
        ),
        in_specs=[pl.BlockSpec(memory_space=pltpu.SMEM)] + [hbm] * 5,
        out_specs=(hbm,) * 4,
        scratch_shapes=[
            vm((GROUP, tok, HD), BF),
            vm((GROUP, HD, tok), BF),
            vm((REACH, tok, HD), BF),
            vm((REACH, tok, HD), BF),
            vm((REACH, HD, tok), BF),
            vm((REACH, HD, tok), BF),
            vm((PARTS, width // PARTS, feat), BF),
            vm((PARTS, width // PARTS, feat), BF),
            vm((2, row, feat), BF),
            vm((GROUP, HD, tok), F32),
            vm((GROUP, 1, tok), F32),
            vm((GROUP, 1, tok), F32),
            vm((GROUP, HD, tok), BF),
            vm((tok, width), BF),
            vm((2, two, width), BF),
            vm((row, feat), BF),
            vm((row, feat), BF),
            vm((row, feat), F32),
            vm((row, feat), BF),
            vm((width, row), F32),
            vm((2, width, row), F32),
            vm((2, width, two), F32),
            vm((2, GROUP, HD, two), BF),
            vm((2, GROUP, HD, two), BF),
            vm((GROUP, HD, tok), BF),
            vm((GROUP, tok, HD), BF),
            vm((GROUP, 1, tok), F32),
            vm((REACH, tok, HD), F32),
            vm((REACH, tok, HD), F32),
            vm((GROUP, HD, tok), F32),
            vm((REACH - 1, tok, 2 * HD), BF),
            vm((REACH, tok, 2 * HD), BF),
            vm((tok, width), BF),
            vm((tok, HD), BF),
            vm((tok, HD), BF),
            vm((1, tok), jnp.int32),
            dma((4 + N_TP * GROUP,)),
            dma((16,)),
            dma((96,)),
            dma((96,)),
        ],
        compiler_params=pltpu.CompilerParams(
            collective_id=0, has_side_effects=True, vmem_limit_bytes=56 * 1024 * 1024
        ),
        cost_estimate=pl.CostEstimate(flops=flops, bytes_accessed=1 << 24, transcendentals=1 << 23),
    )(
        lengths,
        queries,
        key_vectors,
        value_vectors,
        out_weight.reshape(PARTS, width // PARTS, feat),
        grad_output,
    )
    return pl.pallas_call(
        settle,
        out_shape=tuple(jax.ShapeDtypeStruct(a.shape, a.dtype) for a in found),
        in_specs=[hbm] * 4,
        out_specs=(hbm,) * 4,
        scratch_shapes=[vm(a.shape, a.dtype) for a in found] + [dma((2, 4))],
    )(*found)


def solution(mesh):
    return jax.shard_map(
        functools.partial(on_device, mesh.shape["attn"]),
        mesh=mesh,
        in_specs=(
            P(),
            P("attn", "tp"),
            P("attn", "tp"),
            P("attn", "tp"),
            P("tp", None),
            P(("attn", "tp"), None),
        ),
        out_specs=(P(("attn", "tp"), None), P("attn", "tp"), P("attn", "tp"), P("attn", "tp")),
        check_vma=False,
    )
```

```python
import functools

import jax
import jax.numpy as jnp
from jax import lax
from jax.experimental import pallas as pl
from jax.experimental.pallas import tpu as pltpu
from jax.sharding import PartitionSpec as P

HD = 128
REACH = 4
GROUP = 5
N_TP = 4
PARTS = 8
A_CHUNKS, B_CHUNKS = 4, 2
CHUNKS = A_CHUNKS + B_CHUNKS
Z = 8
NEGATIVE = -1e30
SCALE = HD ** (-0.5)
LOG2E = 1.4426950408889634
MESH = pl.DeviceIdType.MESH
BF, F32 = jnp.bfloat16, jnp.float32


def span_of(h):
    return pl.ds(pl.multiple_of(h * HD, HD), HD)


def each_head(body):
    def step(h, carry):
        body(h)
        return carry

    lax.fori_loop(0, GROUP, step, 0)


def dot(a, b):
    return jnp.dot(a, b, preferred_element_type=F32)


def dot_nt(a, b):
    return lax.dot_general(a, b, (((1,), (1,)), ((), ())), preferred_element_type=F32)


def kernel(
    n,
    docs,
    len_ref,
    q_ref,
    k_ref,
    v_ref,
    w_ref,
    go_ref,
    lo_ref,
    gq_ref,
    gk_ref,
    gv_ref,
    qh,
    qt,
    kb,
    vb,
    kt,
    vt,
    wm,
    wp,
    go,
    acc,
    stat_m,
    stat_l,
    ot,
    o_all,
    op,
    rs_send,
    rs_recv,
    lo_acc,
    dot_own,
    dot_part,
    dot_other,
    dot_send,
    dot_recv,
    dt,
    dd,
    delta,
    dk_acc,
    dv_acc,
    dq_acc,
    dkv_send,
    dkv_recv,
    tabs_ref,
    loc_sem,
    send_sem,
    recv_sem,
):
    tok, width = q_ref.shape
    row = tok // N_TP
    two = 2 * row
    feat = go_ref.shape[1]
    me, y = lax.axis_index("attn"), lax.axis_index("tp")
    step_x = n // 4
    core = lax.rem(me, 2)
    x = me // step_x
    y_a = y + 1 - 2 * lax.rem(y, 2)
    y_b = N_TP - 1 - y
    perm = [y, y_b, y_a, N_TP - 1 - y_a]

    def at(shift):
        return (lax.rem(me + shift + n, n), y)

    dev_a, dev_b = (me, y_a), (me, y_b)
    x_up, x_down = at(step_x), at(-step_x)
    z = lax.rem(me // 2, Z)
    z_up = (me + (lax.rem(z + 1, Z) - z) * 2, y)
    z_down = (me + (lax.rem(z + Z - 1, Z) - z) * 2, y)
    sib = (me + 1 - 2 * core, y)

    def part_of(shift):
        return lax.rem(x + shift + 4, 4) * 2 + core

    partners = [at(1), at(-1)] + [dev_a, dev_b, x_up, x_down]
    partners += [z_up, z_down]
    barrier = pltpu.get_barrier_semaphore()
    for dev in partners:
        pl.semaphore_signal(barrier, inc=1, device_id=dev, device_id_type=MESH)

    def local(i, src, dst):
        c = pltpu.make_async_copy(src, dst, loc_sem.at[i])
        c.start()
        return c

    loc_k = local(0, k_ref, kb.at[0])
    loc_v = local(1, v_ref, vb.at[0])
    loc_q = []
    for s in range(N_TP):
        rows = pl.ds(pl.multiple_of(perm[s] * row, row), row)
        for h in range(GROUP):
            loc_q.append(
                local(
                    2 + s * GROUP + h,
                    q_ref.at[rows, pl.ds(h * HD, HD)],
                    qh.at[h, pl.ds(s * row, row)],
                )
            )
    loc_go = local(2 + N_TP * GROUP, go_ref, go.at[0])
    loc_w = local(3 + N_TP * GROUP, w_ref, wm)

    pl.semaphore_wait(barrier, len(partners))

    used = [0]

    def remote(src, dst, dev):
        i = used[0]
        used[0] += 1
        c = pltpu.make_async_remote_copy(
            src_ref=src,
            dst_ref=dst,
            send_sem=send_sem.at[i],
            recv_sem=recv_sem.at[i],
            device_id=dev,
            device_id_type=MESH,
        )
        c.start()
        return c

    z_base = feat * 11 // 20
    tiles = z_base // 128
    wide = [(tiles + i) // A_CHUNKS * 128 for i in range(A_CHUNKS - 1, -1, -1)]
    wide += [(feat - z_base) // B_CHUNKS] * B_CHUNKS
    cols = [pl.ds(sum(wide[:j]), wide[j]) for j in range(CHUNKS)]
    side = [0] * A_CHUNKS + [1] * B_CHUNKS
    mine, from_down, from_up, from_far = [part_of(s) for s in (0, -1, 1, 2)]
    kv = [None, (remote(k_ref, kb.at[1], at(1)), remote(v_ref, vb.at[1], at(1)))]
    rows_of = [(dev_b, dev_a)[i] for i in side]
    wa, go_in = {}, {}

    def ask_weights(j):
        part = w_ref.at[mine, :, cols[j]]
        wa[j] = remote(part, wp.at[mine, :, cols[j]], dev_a)

    def ask_rows(j):
        go_in[j] = remote(go_ref.at[:, cols[j]], go.at[1, :, cols[j]], rows_of[j])

    z_wide = (feat - z_base) // 2
    z_half = (z_wide + 128) // 256 * 128

    def z_piece(ref, shift, low=0, many=z_wide):
        first_col = pl.multiple_of(z_base + core * z_wide + low, 128)
        return ref.at[lax.rem(z + shift + Z, Z), :, pl.ds(first_col, many)]

    ask_weights(0)
    wb = remote(z_piece(w_ref, 0), z_piece(wp, 0), dev_b)
    ask_weights(1)
    ask_rows(0)
    ask_weights(2)
    ask_weights(3)
    ask_rows(1)
    ask_rows(4)
    ask_rows(2)
    ask_rows(5)
    ask_rows(3)

    z_sibs, z_ups, z_downs = [], [], []

    def z_share(piece):
        z_sibs.append(remote(piece, piece, sib))

    def z_first():
        wb.wait_recv()
        piece = z_piece(wp, 0)
        z_ups.append(remote(piece, piece, z_up))
        z_downs.append(remote(piece, piece, z_down))
        z_share(piece)

    def z_next(hop):
        last = hop == Z // 2 - 1
        z_ups[-1].wait_recv()
        piece = z_piece(wp, -hop)
        part = z_piece(wp, -hop, 0, z_half) if last else piece
        z_ups.append(remote(part, part, z_up))
        z_share(piece)
        z_downs[-1].wait_recv()
        piece = z_piece(wp, hop)
        part = z_piece(wp, hop, z_half, z_wide - z_half) if last else piece
        z_downs.append(remote(part, part, z_down))
        z_share(piece)

    def z_last():
        z_ups[-1].wait_recv()
        z_share(z_piece(wp, Z // 2, 0, z_half))
        z_downs[-1].wait_recv()
        z_share(z_piece(wp, Z // 2, z_half, z_wide - z_half))

    up, down, far = {}, {}, {}
    sibs = [[] for _ in range(A_CHUNKS)]

    def pass_own(j):
        wa[j].wait_recv()
        piece = wp.at[mine, :, cols[j]]
        up[j] = remote(piece, piece, x_up)
        down[j] = remote(piece, piece, x_down)
        sibs[j].append(remote(piece, piece, sib))

    def pass_near(j):
        up[j].wait_recv()
        piece = wp.at[from_down, :, cols[j]]
        if j % 2 == 0:
            far[j] = remote(piece, piece, x_up)
        sibs[j].append(remote(piece, piece, sib))
        down[j].wait_recv()
        piece = wp.at[from_up, :, cols[j]]
        if j % 2 == 1:
            far[j] = remote(piece, piece, x_down)
        sibs[j].append(remote(piece, piece, sib))

    def pass_far(j):
        far[j].wait_recv()
        piece = wp.at[from_far, :, cols[j]]
        sibs[j].append(remote(piece, piece, sib))

    def have(j):
        for c in sibs[j]:
            c.wait_recv()

    def next_keys(o):
        for c in kv[o]:
            c.wait_recv()
        if o < REACH - 1:
            kv.append(
                (
                    remote(kb.at[o], kb.at[o + 1], at(1)),
                    remote(vb.at[o], vb.at[o + 1], at(1)),
                )
            )

    end, first = jnp.int32(0), jnp.int32(0)
    for d in range(docs):
        end = end + len_ref[d]
        first = jnp.where(end <= me, end, first)
    depth = me - first

    def bias(o):
        return jnp.where(o <= depth, 0.0, -NEGATIVE).astype(F32)


    lane = lax.broadcasted_iota(jnp.int32, (1, row), 1)
    for s in range(N_TP):
        tabs_ref[:, s * row : (s + 1) * row] = lane + perm[s] * row

    c2 = SCALE * LOG2E

    for c in loc_q:
        c.wait()

    def turn_q(h, carry):
        qt[h] = qh[h].T
        return carry

    lax.fori_loop(0, GROUP, turn_q, 0)

    def turn_kv(o):
        kt[o] = kb[o].T
        vt[o] = vb[o].T

    def forward(o):
        turn_kv(o)

        def head(h, carry):
            s = dot(kb[o], qt[h])
            if o == 0:
                at_u = lax.broadcasted_iota(jnp.int32, (tok, tok), 0)
                s = jnp.where(at_u <= tabs_ref[...], s, NEGATIVE)
                new = jnp.max(s, axis=0, keepdims=True)
                p = jnp.exp2((s - new) * c2)
                stat_l[h] = jnp.sum(p, axis=0, keepdims=True)
                acc[h] = dot(vt[o], p.astype(BF))
            else:
                old = stat_m[h]
                new = jnp.maximum(old, jnp.max(s, axis=0, keepdims=True) - bias(o))
                fade = jnp.exp2((old - new) * c2)
                p = jnp.exp2((s - (new + bias(o))) * c2)
                stat_l[h] = stat_l[h] * fade + jnp.sum(p, axis=0, keepdims=True)
                acc[h] = acc[h] * fade + dot(vt[o], p.astype(BF))
            stat_m[h] = new
            return carry

        lax.fori_loop(0, GROUP, head, 0, unroll=o > 0)

    loc_k.wait()
    loc_v.wait()
    forward(0)
    next_keys(1)
    z_first()
    pass_own(0)
    forward(1)
    pass_own(1)
    next_keys(2)
    forward(2)
    pass_own(2)
    z_next(1)
    next_keys(3)
    forward(3)
    pass_own(3)

    def finish(h):
        low = (acc[h] * (1.0 / stat_l[h])).astype(BF)
        ot[h] = low
        o_all[:, span_of(h)] = low.T
        stat_l[h] = stat_m[h] * c2 + jnp.log2(stat_l[h])

    each_head(finish)
    o_in = [
        remote(o_all.at[pl.ds(two, two)], op.at[0], dev_a),
        remote(o_all.at[pl.ds(row, row)], op.at[1, pl.ds(0, row)], dev_b),
        remote(o_all.at[pl.ds(3 * row, row)], op.at[1, pl.ds(row, row)], dev_b),
    ]
    def weights(w3, j):
        return w3[:, :, cols[j]].reshape(width, wide[j])

    def add_to(total, part, fresh):
        if fresh:
            total[...] = part
        else:
            total[...] += part

    def cotangent_own():
        for j in range(CHUNKS):
            add_to(dot_own, dot_nt(weights(wm, j), go[0, :, cols[j]]), j == 0)

    def cotangent_rows(j):
        fresh = j in (0, A_CHUNKS)
        add_to(dot_part.at[side[j]], dot_nt(weights(wm, j), go[1, :, cols[j]]), fresh)

    def cotangent_other(j):
        both = go[:, :, cols[j]].reshape(two, wide[j])
        add_to(dot_other.at[side[j]], dot_nt(weights(wp, j), both), j in (0, A_CHUNKS))

    def send_cotangent(i):
        def low(h):
            dot_send[i, h] = dot_other[i, span_of(h), :].astype(BF)

        each_head(low)
        return remote(dot_send.at[i], dot_recv.at[i], [dev_a, dev_b][i])

    rs = {}

    def project(j):
        if side[j] == 0:
            mine_o, other_o = o_all[0:two], op[0]
        else:
            mine_o = jnp.concatenate([o_all[0:row], o_all[two : two + row]], axis=0)
            other_o = op[1]
        one = dot(mine_o, weights(wm, j)).astype(BF)
        other = dot(other_o, weights(wp, j)).astype(BF)
        both = one.astype(F32) + other.astype(F32)
        lo_acc[:, cols[j]] = both[0:row]
        rs_send[:, cols[j]] = both[row:two].astype(BF)

    def send_rows(j):
        rs[j] = remote(rs_send.at[:, cols[j]], rs_recv.at[:, cols[j]], rows_of[j])

    def turn_d(h, base, size, high):
        dt[h, :, base : base + size] = high
        dd[h, base : base + size] = high.T
        delta[h, :, base : base + size] = jnp.sum(
            high.astype(F32) * ot[h, :, base : base + size].astype(F32), axis=0, keepdims=True
        )

    def turn_own():
        each_head(lambda h: turn_d(h, 0, row, dot_own[span_of(h), :].astype(BF)))

    def turn_rest():
        def head(h):
            from_a, from_b = dot_recv[0, h].astype(F32), dot_recv[1, h].astype(F32)
            turn_d(h, row, row, (dot_part[0, span_of(h)] + from_b[:, 0:row]).astype(BF))
            turn_d(h, two, row, (dot_part[1, span_of(h)] + from_a[:, 0:row]).astype(BF))
            turn_d(h, 3 * row, row, (from_a[:, row:two] + from_b[:, row:two]).astype(BF))

        each_head(head)

    def backward(o, base, size):
        tl = slice(base, base + size)
        out = bias(o)

        def head(h):
            s = dot(kb[o], qt[h, :, tl])
            p = jnp.exp2(s * c2 - (stat_l[h, :, tl] + out))
            if base == 0 or (isinstance(o, int) and o == 0):
                at_u = lax.broadcasted_iota(jnp.int32, (tok, size), 0)
                p = jnp.where(at_u <= tabs_ref[:, tl] + jnp.where(o > 0, tok, 0), p, 0.0)
            dp = dot(vb[o], dt[h, :, tl])
            ds = (p * (dp - delta[h, :, tl])).astype(BF)
            part_v, part_k = dot(p.astype(BF), dd[h, tl]), dot(ds, qh[h, tl])
            if base == 0 and h == 0:
                dv_acc[o] = part_v
                dk_acc[o] = part_k
            else:
                dv_acc[o] += part_v
                dk_acc[o] += part_k
            dq_acc[h, :, tl] += dot(kt[o], ds)

        for h in range(GROUP):
            head(h)

    def own_rows(i, carry):
        backward(REACH - 1 - i, 0, row)
        return carry

    dq_acc[...] = jnp.zeros_like(dq_acc)
    dkv_recv[REACH - 1] = jnp.zeros((tok, 2 * HD), BF)

    pass_near(0)
    pass_near(1)
    loc_w.wait()
    loc_go.wait()
    cotangent_own()
    turn_own()
    z_next(2)
    lax.fori_loop(0, 2, own_rows, 0)
    pass_near(2)
    pass_near(3)
    for j in (0, 1):
        go_in[j].wait_recv()
        cotangent_rows(j)
    z_next(3)
    for j in (2, 3, 4, 5):
        go_in[j].wait_recv()
        cotangent_rows(j)
    for j in range(A_CHUNKS):
        pass_far(j)
    z_last()
    for j in range(A_CHUNKS):
        have(j)
        cotangent_other(j)
    d_in = [send_cotangent(0)]
    for c in z_sibs:
        c.wait_recv()
    cotangent_other(4)
    cotangent_other(5)
    d_in.append(send_cotangent(1))
    o_in[0].wait_recv()
    for j in (0, 1):
        project(j)
        send_rows(j)
    o_in[1].wait_recv()
    o_in[2].wait_recv()
    for j in (4, 2, 5, 3):
        project(j)
        send_rows(j)
    lax.fori_loop(2, REACH, own_rows, 0)
    for c in d_in:
        c.wait_recv()
    turn_rest()

    back_at = used[0]

    def back_copy(o):
        i = back_at + o
        c = pltpu.make_async_remote_copy(
            src_ref=dkv_send.at[o - 1],
            dst_ref=dkv_recv.at[o - 1],
            send_sem=send_sem.at[i],
            recv_sem=recv_sem.at[i],
            device_id=at(-1),
            device_id_type=MESH,
        )
        return c

    def sums(o):
        gk = dk_acc[o] * SCALE + dkv_recv[o, :, 0:HD].astype(F32)
        gv = dv_acc[o] + dkv_recv[o, :, HD : 2 * HD].astype(F32)
        return gk.astype(BF), gv.astype(BF)

    def other_rows(i, carry):
        o = REACH - 1 - i
        backward(o, row, tok - row)

        @pl.when(o < REACH - 1)
        def _():
            back_copy(o + 1).wait_recv()

        gk, gv = sums(o)
        dkv_send[o - 1, :, 0:HD] = gk
        dkv_send[o - 1, :, HD : 2 * HD] = gv
        back_copy(o).start()
        return carry

    lax.fori_loop(0, REACH - 1, other_rows, 0)
    backward(0, row, tok - row)

    def put_queries(h):
        for s in range(N_TP):
            rows = pl.ds(pl.multiple_of(perm[s] * row, row), row)
            part = dq_acc[h, :, s * row : (s + 1) * row] * SCALE
            gq_ref[rows, span_of(h)] = part.T.astype(BF)

    each_head(put_queries)
    back_copy(1).wait_recv()
    gk_ref[...], gv_ref[...] = sums(0)
    for j in range(CHUNKS):
        rs[j].wait_recv()
        lo_ref[:, cols[j]] = (lo_acc[:, cols[j]] + rs_recv[:, cols[j]].astype(F32)).astype(BF)

    sent = [c for pair in kv[1:] for c in pair] + o_in + d_in
    sent += [back_copy(o) for o in range(1, REACH)]
    sent += [wb] + z_sibs + z_ups + z_downs
    for j in range(CHUNKS):
        sent += [go_in[j], rs[j]]
    for j in range(A_CHUNKS):
        sent += [wa[j], up[j], down[j], far[j]] + sibs[j]
    for c in sent:
        c.wait_send()


def settle(*refs):
    many = len(refs) // 2
    copies = [pltpu.make_async_copy(refs[i], refs[many + i], refs[-1].at[i]) for i in range(many)]
    for c in copies:
        c.start()
    for c in copies:
        c.wait()


def on_device(n, lengths, queries, key_vectors, value_vectors, out_weight, grad_output):
    tok, width = queries.shape
    feat = out_weight.shape[1]
    row, two = tok // N_TP, tok // 2
    docs = lengths.shape[0]
    hbm = pl.BlockSpec(memory_space=pl.ANY)
    vm = pltpu.VMEM
    dma = pltpu.SemaphoreType.DMA
    flops = 2 * tok * width * feat * 2 + 7 * 2 * tok * tok * width * REACH
    found = pl.pallas_call(
        functools.partial(kernel, n, docs),
        out_shape=(
            vm((row, feat), BF),
            vm((tok, width), BF),
            vm((tok, HD), BF),
            vm((tok, HD), BF),
        ),
        in_specs=[pl.BlockSpec(memory_space=pltpu.SMEM)] + [hbm] * 5,
        out_specs=(pl.BlockSpec(memory_space=pltpu.VMEM),) * 4,
        scratch_shapes=[
            vm((GROUP, tok, HD), BF),
            vm((GROUP, HD, tok), BF),
            vm((REACH, tok, HD), BF),
            vm((REACH, tok, HD), BF),
            vm((REACH, HD, tok), BF),
            vm((REACH, HD, tok), BF),
            vm((PARTS, width // PARTS, feat), BF),
            vm((PARTS, width // PARTS, feat), BF),
            vm((2, row, feat), BF),
            vm((GROUP, HD, tok), F32),
            vm((GROUP, 1, tok), F32),
            vm((GROUP, 1, tok), F32),
            vm((GROUP, HD, tok), BF),
            vm((tok, width), BF),
            vm((2, two, width), BF),
            vm((row, feat), BF),
            vm((row, feat), BF),
            vm((row, feat), F32),
            vm((width, row), F32),
            vm((2, width, row), F32),
            vm((2, width, two), F32),
            vm((2, GROUP, HD, two), BF),
            vm((2, GROUP, HD, two), BF),
            vm((GROUP, HD, tok), BF),
            vm((GROUP, tok, HD), BF),
            vm((GROUP, 1, tok), F32),
            vm((REACH, tok, HD), F32),
            vm((REACH, tok, HD), F32),
            vm((GROUP, HD, tok), F32),
            vm((REACH - 1, tok, 2 * HD), BF),
            vm((REACH, tok, 2 * HD), BF),
            vm((1, tok), jnp.int32),
            dma((4 + N_TP * GROUP,)),
            dma((96,)),
            dma((96,)),
        ],
        compiler_params=pltpu.CompilerParams(
            collective_id=0, has_side_effects=True, vmem_limit_bytes=56 * 1024 * 1024
        ),
        cost_estimate=pl.CostEstimate(flops=flops, bytes_accessed=1 << 24, transcendentals=1 << 23),
    )(
        lengths,
        queries,
        key_vectors,
        value_vectors,
        out_weight.reshape(PARTS, width // PARTS, feat),
        grad_output,
    )
    return pl.pallas_call(
        settle,
        out_shape=tuple(jax.ShapeDtypeStruct(a.shape, a.dtype) for a in found),
        in_specs=[pl.BlockSpec(memory_space=pltpu.VMEM)] * 4,
        out_specs=(hbm,) * 4,
        scratch_shapes=[dma((4,))],
    )(*found)


def solution(mesh):
    return jax.shard_map(
        functools.partial(on_device, mesh.shape["attn"]),
        mesh=mesh,
        in_specs=(
            P(),
            P("attn", "tp"),
            P("attn", "tp"),
            P("attn", "tp"),
            P("tp", None),
            P(("attn", "tp"), None),
        ),
        out_specs=(P(("attn", "tp"), None), P("attn", "tp"), P("attn", "tp"), P("attn", "tp")),
        check_vma=False,
    )
```

```python
import functools

import jax
import jax.numpy as jnp
from jax import lax
from jax.experimental import pallas as pl
from jax.experimental.pallas import tpu as pltpu
from jax.sharding import PartitionSpec as P

HD = 128
REACH = 4
GROUP = 5
N_TP = 4
PARTS = 8
A_CHUNKS, B_CHUNKS = 4, 2
CHUNKS = A_CHUNKS + B_CHUNKS
Z = 8
NEGATIVE = -1e30
SCALE = HD ** (-0.5)
LOG2E = 1.4426950408889634
MESH = pl.DeviceIdType.MESH
BF, F32 = jnp.bfloat16, jnp.float32


def dot(a, b):
    return jnp.dot(a, b, preferred_element_type=F32)


def dot_nt(a, b):
    return lax.dot_general(a, b, (((1,), (1,)), ((), ())), preferred_element_type=F32)


def kernel(
    n,
    docs,
    len_ref,
    q_ref,
    k_ref,
    v_ref,
    w_ref,
    go_ref,
    lo_ref,
    gq_ref,
    gk_ref,
    gv_ref,
    qh,
    qt,
    kb,
    vb,
    kt,
    vt,
    wm,
    wp,
    go,
    acc,
    stat_m,
    stat_l,
    ot,
    o_all,
    op,
    rs_send,
    rs_recv,
    lo_acc,
    lo_out,
    dot_own,
    dot_part,
    dot_other,
    dot_send,
    dot_recv,
    dt,
    dd,
    delta,
    dk_acc,
    dv_acc,
    dq_acc,
    dkv_send,
    dkv_recv,
    gq_out,
    gk_out,
    gv_out,
    tabs_ref,
    loc_sem,
    out_sem,
    send_sem,
    recv_sem,
):
    tok, width = q_ref.shape
    row = tok // N_TP
    two = 2 * row
    feat = go_ref.shape[1]
    me, y = lax.axis_index("attn"), lax.axis_index("tp")
    step_x = n // 4
    core = lax.rem(me, 2)
    x = me // step_x
    y_a = y + 1 - 2 * lax.rem(y, 2)
    y_b = N_TP - 1 - y
    perm = [y, y_b, y_a, N_TP - 1 - y_a]

    def at(shift):
        return (lax.rem(me + shift + n, n), y)

    dev_a, dev_b = (me, y_a), (me, y_b)
    x_up, x_down = at(step_x), at(-step_x)
    z = lax.rem(me // 2, Z)
    z_up = (me + (lax.rem(z + 1, Z) - z) * 2, y)
    z_down = (me + (lax.rem(z + Z - 1, Z) - z) * 2, y)
    sib = (me + 1 - 2 * core, y)

    def part_of(shift):
        return lax.rem(x + shift + 4, 4) * 2 + core

    partners = [at(1), at(-1)] + [dev_a, dev_b, x_up, x_down]
    partners += [z_up, z_down]
    barrier = pltpu.get_barrier_semaphore()
    for dev in partners:
        pl.semaphore_signal(barrier, inc=1, device_id=dev, device_id_type=MESH)

    def local(i, src, dst):
        c = pltpu.make_async_copy(src, dst, loc_sem.at[i])
        c.start()
        return c

    loc_k = local(0, k_ref, kb.at[0])
    loc_v = local(1, v_ref, vb.at[0])
    loc_q = []
    for s in range(N_TP):
        rows = pl.ds(pl.multiple_of(perm[s] * row, row), row)
        for h in range(GROUP):
            loc_q.append(
                local(
                    2 + s * GROUP + h,
                    q_ref.at[rows, pl.ds(h * HD, HD)],
                    qh.at[h, pl.ds(s * row, row)],
                )
            )
    loc_go = local(2 + N_TP * GROUP, go_ref, go.at[0])
    loc_w = local(3 + N_TP * GROUP, w_ref, wm)

    pl.semaphore_wait(barrier, len(partners))

    used = [0]

    def remote(src, dst, dev):
        i = used[0]
        used[0] += 1
        c = pltpu.make_async_remote_copy(
            src_ref=src,
            dst_ref=dst,
            send_sem=send_sem.at[i],
            recv_sem=recv_sem.at[i],
            device_id=dev,
            device_id_type=MESH,
        )
        c.start()
        return c

    z_base = feat * 3 // 5
    wide = [z_base // A_CHUNKS] * A_CHUNKS + [(feat - z_base) // B_CHUNKS] * B_CHUNKS
    cols = [pl.ds(sum(wide[:j]), wide[j]) for j in range(CHUNKS)]
    side = [0] * A_CHUNKS + [1] * B_CHUNKS
    mine, from_down, from_up, from_far = [part_of(s) for s in (0, -1, 1, 2)]
    kv = [None, (remote(k_ref, kb.at[1], at(1)), remote(v_ref, vb.at[1], at(1)))]
    rows_of = [(dev_b, dev_a)[i] for i in side]
    wa, go_in = {}, {}

    def ask_weights(j):
        part = w_ref.at[mine, :, cols[j]]
        wa[j] = remote(part, wp.at[mine, :, cols[j]], dev_a)

    def ask_rows(j):
        go_in[j] = remote(go_ref.at[:, cols[j]], go.at[1, :, cols[j]], rows_of[j])

    z_wide = (feat - z_base) // Z

    def z_piece(ref, shift, low=0, many=PARTS // 2):
        first_col = pl.multiple_of(z_base + lax.rem(z + shift + Z, Z) * z_wide, z_wide)
        return ref.at[pl.ds(core * (PARTS // 2) + low, many), :, pl.ds(first_col, z_wide)]

    ask_weights(0)
    wb = remote(z_piece(w_ref, 0), z_piece(wp, 0), dev_b)
    ask_weights(1)
    ask_rows(0)
    ask_weights(2)
    ask_weights(3)
    ask_rows(1)
    ask_rows(4)
    ask_rows(2)
    ask_rows(3)

    z_sibs, z_ups, z_downs = [], [], []

    def z_share(piece):
        z_sibs.append(remote(piece, piece, sib))

    def z_first():
        wb.wait_recv()
        piece = z_piece(wp, 0)
        z_ups.append(remote(piece, piece, z_up))
        z_downs.append(remote(piece, piece, z_down))
        z_share(piece)

    def z_next(hop):
        last = hop == Z // 2 - 1
        z_ups[-1].wait_recv()
        piece = z_piece(wp, -hop)
        part = z_piece(wp, -hop, 0, PARTS // 4) if last else piece
        z_ups.append(remote(part, part, z_up))
        z_share(piece)
        z_downs[-1].wait_recv()
        piece = z_piece(wp, hop)
        part = z_piece(wp, hop, PARTS // 4, PARTS // 4) if last else piece
        z_downs.append(remote(part, part, z_down))
        z_share(piece)

    def z_last():
        z_ups[-1].wait_recv()
        z_share(z_piece(wp, Z // 2, 0, PARTS // 4))
        z_downs[-1].wait_recv()
        z_share(z_piece(wp, Z // 2, PARTS // 4, PARTS // 4))

    up, down, far = {}, {}, {}
    sibs = [[] for _ in range(A_CHUNKS)]

    def pass_own(j):
        wa[j].wait_recv()
        piece = wp.at[mine, :, cols[j]]
        up[j] = remote(piece, piece, x_up)
        down[j] = remote(piece, piece, x_down)
        sibs[j].append(remote(piece, piece, sib))

    def pass_near(j):
        up[j].wait_recv()
        piece = wp.at[from_down, :, cols[j]]
        if j % 2 == 0:
            far[j] = remote(piece, piece, x_up)
        sibs[j].append(remote(piece, piece, sib))
        down[j].wait_recv()
        piece = wp.at[from_up, :, cols[j]]
        if j % 2 == 1:
            far[j] = remote(piece, piece, x_down)
        sibs[j].append(remote(piece, piece, sib))

    def pass_far(j):
        far[j].wait_recv()
        piece = wp.at[from_far, :, cols[j]]
        sibs[j].append(remote(piece, piece, sib))

    def have(j):
        for c in sibs[j]:
            c.wait_recv()

    def next_keys(o):
        for c in kv[o]:
            c.wait_recv()
        if o < REACH - 1:
            kv.append(
                (
                    remote(kb.at[o], kb.at[o + 1], at(1)),
                    remote(vb.at[o], vb.at[o + 1], at(1)),
                )
            )

    end, first = jnp.int32(0), jnp.int32(0)
    for d in range(docs):
        end = end + len_ref[d]
        first = jnp.where(end <= me, end, first)
    depth = me - first

    def bias(o):
        return jnp.where(o <= depth, 0.0, -NEGATIVE).astype(F32)


    lane = lax.broadcasted_iota(jnp.int32, (1, row), 1)
    for s in range(N_TP):
        tabs_ref[:, s * row : (s + 1) * row] = lane + perm[s] * row

    c2 = SCALE * LOG2E

    for c in loc_q:
        c.wait()

    def turn_q(h, carry):
        qt[h] = qh[h].T
        return carry

    lax.fori_loop(0, GROUP, turn_q, 0)

    def turn_kv(o):
        kt[o] = kb[o].T
        vt[o] = vb[o].T

    def forward(o):
        turn_kv(o)

        def head(h, carry):
            s = dot(kb[o], qt[h])
            if o == 0:
                at_u = lax.broadcasted_iota(jnp.int32, (tok, tok), 0)
                s = jnp.where(at_u <= tabs_ref[...], s, NEGATIVE)
                new = jnp.max(s, axis=0, keepdims=True)
                p = jnp.exp2((s - new) * c2)
                stat_l[h] = jnp.sum(p, axis=0, keepdims=True)
                acc[h] = dot(vt[o], p.astype(BF))
            else:
                old = stat_m[h]
                new = jnp.maximum(old, jnp.max(s, axis=0, keepdims=True) - bias(o))
                fade = jnp.exp2((old - new) * c2)
                p = jnp.exp2((s - (new + bias(o))) * c2)
                stat_l[h] = stat_l[h] * fade + jnp.sum(p, axis=0, keepdims=True)
                acc[h] = acc[h] * fade + dot(vt[o], p.astype(BF))
            stat_m[h] = new

        for h in range(GROUP):
            head(h, None)

    loc_k.wait()
    loc_v.wait()
    forward(0)
    next_keys(1)
    z_first()
    pass_own(0)
    forward(1)
    pass_own(1)
    next_keys(2)
    forward(2)
    pass_own(2)
    z_next(1)
    next_keys(3)
    forward(3)
    pass_own(3)

    for h in range(GROUP):
        low = (acc[h] * (1.0 / stat_l[h])).astype(BF)
        ot[h] = low
        o_all[:, h * HD : (h + 1) * HD] = low.T
        stat_l[h] = stat_m[h] * c2 + jnp.log2(stat_l[h])
    o_in = [
        remote(o_all.at[pl.ds(two, two)], op.at[0], dev_a),
        remote(o_all.at[pl.ds(row, row)], op.at[1, pl.ds(0, row)], dev_b),
        remote(o_all.at[pl.ds(3 * row, row)], op.at[1, pl.ds(row, row)], dev_b),
    ]
    ask_rows(5)

    def weights(w3, j):
        return w3[:, :, cols[j]].reshape(width, wide[j])

    def add_to(total, part, fresh):
        if fresh:
            total[...] = part
        else:
            total[...] += part

    def cotangent_own():
        for j in range(CHUNKS):
            add_to(dot_own, dot_nt(weights(wm, j), go[0, :, cols[j]]), j == 0)

    def cotangent_rows(j):
        fresh = j in (0, A_CHUNKS)
        add_to(dot_part.at[side[j]], dot_nt(weights(wm, j), go[1, :, cols[j]]), fresh)

    def cotangent_other(j):
        both = go[:, :, cols[j]].reshape(two, wide[j])
        add_to(dot_other.at[side[j]], dot_nt(weights(wp, j), both), j in (0, A_CHUNKS))

    def send_cotangent(i):
        for h in range(GROUP):
            dot_send[i, h] = dot_other[i, h * HD : (h + 1) * HD, :].astype(BF)
        return remote(dot_send.at[i], dot_recv.at[i], [dev_a, dev_b][i])

    rs = {}

    def project(j):
        if side[j] == 0:
            mine_o, other_o = o_all[0:two], op[0]
        else:
            mine_o = jnp.concatenate([o_all[0:row], o_all[two : two + row]], axis=0)
            other_o = op[1]
        one = dot(mine_o, weights(wm, j)).astype(BF)
        other = dot(other_o, weights(wp, j)).astype(BF)
        both = one.astype(F32) + other.astype(F32)
        lo_acc[:, cols[j]] = both[0:row]
        rs_send[:, cols[j]] = both[row:two].astype(BF)

    def send_rows(j):
        rs[j] = remote(rs_send.at[:, cols[j]], rs_recv.at[:, cols[j]], rows_of[j])

    def turn_d(h, base, size, high):
        dt[h, :, base : base + size] = high
        dd[h, base : base + size] = high.T
        delta[h, :, base : base + size] = jnp.sum(
            high.astype(F32) * ot[h, :, base : base + size].astype(F32), axis=0, keepdims=True
        )

    def turn_own():
        for h in range(GROUP):
            turn_d(h, 0, row, dot_own[h * HD : (h + 1) * HD, :].astype(BF))

    def turn_rest():
        for h in range(GROUP):
            at_h = slice(h * HD, (h + 1) * HD)
            from_a, from_b = dot_recv[0, h].astype(F32), dot_recv[1, h].astype(F32)
            turn_d(h, row, row, (dot_part[0, at_h] + from_b[:, 0:row]).astype(BF))
            turn_d(h, two, row, (dot_part[1, at_h] + from_a[:, 0:row]).astype(BF))
            turn_d(h, 3 * row, row, (from_a[:, row:two] + from_b[:, row:two]).astype(BF))

    def backward(o, base, size):
        tl = slice(base, base + size)
        out = bias(o)

        def head(h):
            s = dot(kb[o], qt[h, :, tl])
            p = jnp.exp2(s * c2 - (stat_l[h, :, tl] + out))
            if base == 0 or (isinstance(o, int) and o == 0):
                at_u = lax.broadcasted_iota(jnp.int32, (tok, size), 0)
                p = jnp.where(at_u <= tabs_ref[:, tl] + jnp.where(o > 0, tok, 0), p, 0.0)
            dp = dot(vb[o], dt[h, :, tl])
            ds = (p * (dp - delta[h, :, tl])).astype(BF)
            part_v, part_k = dot(p.astype(BF), dd[h, tl]), dot(ds, qh[h, tl])
            if base == 0 and h == 0:
                dv_acc[o] = part_v
                dk_acc[o] = part_k
            else:
                dv_acc[o] += part_v
                dk_acc[o] += part_k
            dq_acc[h, :, tl] += dot(kt[o], ds)

        for h in range(GROUP):
            head(h)

    def own_rows(i, carry):
        backward(REACH - 1 - i, 0, row)
        return carry

    dq_acc[...] = jnp.zeros_like(dq_acc)
    dkv_recv[REACH - 1] = jnp.zeros((tok, 2 * HD), BF)

    pass_near(0)
    pass_near(1)
    loc_w.wait()
    loc_go.wait()
    cotangent_own()
    turn_own()
    z_next(2)
    lax.fori_loop(0, 2, own_rows, 0)
    pass_near(2)
    pass_near(3)
    for j in (0, 1):
        go_in[j].wait_recv()
        cotangent_rows(j)
    z_next(3)
    for j in (2, 3, 4):
        go_in[j].wait_recv()
        cotangent_rows(j)
    for j in range(A_CHUNKS):
        pass_far(j)
    z_last()
    for j in range(A_CHUNKS):
        have(j)
        cotangent_other(j)
    d_in = [send_cotangent(0)]
    o_in[0].wait_recv()
    project(0)
    send_rows(0)
    for c in z_sibs:
        c.wait_recv()
    cotangent_other(4)
    go_in[5].wait_recv()
    cotangent_other(5)
    d_in.append(send_cotangent(1))
    project(1)
    send_rows(1)
    cotangent_rows(5)
    o_in[1].wait_recv()
    o_in[2].wait_recv()
    for j in (4, 2, 5, 3):
        project(j)
        send_rows(j)
    lax.fori_loop(2, REACH, own_rows, 0)
    for c in d_in:
        c.wait_recv()
    turn_rest()

    back_at = used[0]

    def back_copy(o):
        i = back_at + o
        c = pltpu.make_async_remote_copy(
            src_ref=dkv_send.at[o - 1],
            dst_ref=dkv_recv.at[o - 1],
            send_sem=send_sem.at[i],
            recv_sem=recv_sem.at[i],
            device_id=at(-1),
            device_id_type=MESH,
        )
        return c

    def sums(o):
        gk = dk_acc[o] * SCALE + dkv_recv[o, :, 0:HD].astype(F32)
        gv = dv_acc[o] + dkv_recv[o, :, HD : 2 * HD].astype(F32)
        return gk.astype(BF), gv.astype(BF)

    def other_rows(i, carry):
        o = REACH - 1 - i
        backward(o, row, tok - row)

        @pl.when(o < REACH - 1)
        def _():
            back_copy(o + 1).wait_recv()

        gk, gv = sums(o)
        dkv_send[o - 1, :, 0:HD] = gk
        dkv_send[o - 1, :, HD : 2 * HD] = gv
        back_copy(o).start()
        return carry

    lax.fori_loop(0, REACH - 1, other_rows, 0)
    backward(0, row, tok - row)

    outs = []

    def put(src, dst):
        c = pltpu.make_async_copy(src, dst, out_sem.at[len(outs)])
        c.start()
        outs.append(c)

    for h in range(GROUP):
        gq_out[:, h * HD : (h + 1) * HD] = (dq_acc[h] * SCALE).T.astype(BF)
    for s in range(N_TP):
        rows = pl.ds(pl.multiple_of(perm[s] * row, row), row)
        put(gq_out.at[pl.ds(s * row, row)], gq_ref.at[rows])

    for j in range(CHUNKS):
        rs[j].wait_recv()
        lo_out[:, cols[j]] = (lo_acc[:, cols[j]] + rs_recv[:, cols[j]].astype(F32)).astype(BF)
        put(lo_out.at[:, cols[j]], lo_ref.at[:, cols[j]])

    back_copy(1).wait_recv()
    gk_out[...], gv_out[...] = sums(0)
    put(gk_out, gk_ref)
    put(gv_out, gv_ref)

    sent = [c for pair in kv[1:] for c in pair] + o_in + d_in
    sent += [back_copy(o) for o in range(1, REACH)]
    sent += [wb] + z_sibs + z_ups + z_downs
    for j in range(CHUNKS):
        sent += [go_in[j], rs[j]]
    for j in range(A_CHUNKS):
        sent += [wa[j], up[j], down[j], far[j]] + sibs[j]
    for c in sent:
        c.wait_send()
    for c in outs:
        c.wait()


def settle(*refs):
    many = len(refs) // 3
    came, went, held, sems = refs[:many], refs[many : 2 * many], refs[2 * many : -1], refs[-1]
    loads = [pltpu.make_async_copy(came[i], held[i], sems.at[0, i]) for i in range(many)]
    stores = [pltpu.make_async_copy(held[i], went[i], sems.at[1, i]) for i in range(many)]
    for c in loads:
        c.start()
    for load, store in zip(loads, stores):
        load.wait()
        store.start()
    for c in stores:
        c.wait()


def on_device(n, lengths, queries, key_vectors, value_vectors, out_weight, grad_output):
    tok, width = queries.shape
    feat = out_weight.shape[1]
    row, two = tok // N_TP, tok // 2
    docs = lengths.shape[0]
    hbm = pl.BlockSpec(memory_space=pl.ANY)
    vm = pltpu.VMEM
    dma = pltpu.SemaphoreType.DMA
    flops = 2 * tok * width * feat * 2 + 7 * 2 * tok * tok * width * REACH
    found = pl.pallas_call(
        functools.partial(kernel, n, docs),
        out_shape=(
            jax.ShapeDtypeStruct((row, feat), BF),
            jax.ShapeDtypeStruct((tok, width), BF),
            jax.ShapeDtypeStruct((tok, HD), BF),
            jax.ShapeDtypeStruct((tok, HD), BF),
        ),
        in_specs=[pl.BlockSpec(memory_space=pltpu.SMEM)] + [hbm] * 5,
        out_specs=(hbm,) * 4,
        scratch_shapes=[
            vm((GROUP, tok, HD), BF),
            vm((GROUP, HD, tok), BF),
            vm((REACH, tok, HD), BF),
            vm((REACH, tok, HD), BF),
            vm((REACH, HD, tok), BF),
            vm((REACH, HD, tok), BF),
            vm((PARTS, width // PARTS, feat), BF),
            vm((PARTS, width // PARTS, feat), BF),
            vm((2, row, feat), BF),
            vm((GROUP, HD, tok), F32),
            vm((GROUP, 1, tok), F32),
            vm((GROUP, 1, tok), F32),
            vm((GROUP, HD, tok), BF),
            vm((tok, width), BF),
            vm((2, two, width), BF),
            vm((row, feat), BF),
            vm((row, feat), BF),
            vm((row, feat), F32),
            vm((row, feat), BF),
            vm((width, row), F32),
            vm((2, width, row), F32),
            vm((2, width, two), F32),
            vm((2, GROUP, HD, two), BF),
            vm((2, GROUP, HD, two), BF),
            vm((GROUP, HD, tok), BF),
            vm((GROUP, tok, HD), BF),
            vm((GROUP, 1, tok), F32),
            vm((REACH, tok, HD), F32),
            vm((REACH, tok, HD), F32),
            vm((GROUP, HD, tok), F32),
            vm((REACH - 1, tok, 2 * HD), BF),
            vm((REACH, tok, 2 * HD), BF),
            vm((tok, width), BF),
            vm((tok, HD), BF),
            vm((tok, HD), BF),
            vm((1, tok), jnp.int32),
            dma((4 + N_TP * GROUP,)),
            dma((16,)),
            dma((96,)),
            dma((96,)),
        ],
        compiler_params=pltpu.CompilerParams(
            collective_id=0, has_side_effects=True, vmem_limit_bytes=56 * 1024 * 1024
        ),
        cost_estimate=pl.CostEstimate(flops=flops, bytes_accessed=1 << 24, transcendentals=1 << 23),
    )(
        lengths,
        queries,
        key_vectors,
        value_vectors,
        out_weight.reshape(PARTS, width // PARTS, feat),
        grad_output,
    )
    return pl.pallas_call(
        settle,
        out_shape=tuple(jax.ShapeDtypeStruct(a.shape, a.dtype) for a in found),
        in_specs=[hbm] * 4,
        out_specs=(hbm,) * 4,
        scratch_shapes=[vm(a.shape, a.dtype) for a in found] + [dma((2, 4))],
    )(*found)


def solution(mesh):
    return jax.shard_map(
        functools.partial(on_device, mesh.shape["attn"]),
        mesh=mesh,
        in_specs=(
            P(),
            P("attn", "tp"),
            P("attn", "tp"),
            P("attn", "tp"),
            P("tp", None),
            P(("attn", "tp"), None),
        ),
        out_specs=(P(("attn", "tp"), None), P("attn", "tp"), P("attn", "tp"), P("attn", "tp")),
        check_vma=False,
    )
```
